32 devices in a mesh: sea: 2 (over x), body: 4 (over z), harm: 4 (over y, core).
Axes of the slice: x: 2, y: 2, z: 4, core: 2. Of those that a mesh axis runs over, the one named last changes fastest.
Arguments:
- vel: float32 [2, 128, 256, 128], P(None, 'harm', 'body', 'sea'), parts along dimension 3, may hold values from -4 to 4
- imped: bfloat16 [2, 128, 256, 256], P(None, 'harm', 'body'), may hold values from -3 to 3, as said below
- excite: float32 [2, 128, 256, 128], P(None, 'harm', 'body', 'sea'), parts along dimension 3, may hold values from -16 to 16
- quad_coef: float32 [256], P('body'), may hold values from 0.3 to 3
- coul_coef: float32 [256], P('body'), may hold values from 0.3 to 3
Outputs:
- vel_new: float32 [2, 128, 256, 128], P(None, 'harm', 'body', 'sea'), parts along dimension 3
- rms: float32 [2], P('sea'), parts along dimension 0
The draws below stay inside these ranges and needn't reach their ends.
There are 2 independent parts, one for each index of `sea`. The reference program is written for one: setup_inputs(seed, part) draws one part's arguments, and reference() takes and returns one part's arrays. A program takes and returns all parts, laid end to end along the dimension named above; an argument that names none is the same for every part. Nothing has to cross between parts.
Inputs may be any that keep to these rules, and one draw needn't show every extreme that they name: imped[c, h, a, b] equals imped[c, h, b, a] for all c, h, a, b, and every diagonal real part imped[0, h, b, b] lies between 1 and 3.
All inputs are finite; a program needn't handle non-finite values.
Results may differ from the reference program's by a relative error of at most 0.0039.
Values may be sent and summed in bfloat16 or wider, within the bound.
No kernel may reach another device: no remote copies, remote signals or barrier semaphores. Data moves between devices by JAX's collectives and lax.ppermute only.
A program may use at most 192 MiB of HBM per device.

```python
import math
import jax
import jax.numpy as jnp
from jax import lax

REALS = 64
H = 128
NT = 512
BODIES = 256


def draw_imped(key, part):
    key_off, key_re, key_im = jax.random.split(key, 3)
    raw_values = jnp.clip(jax.random.normal(key_off, (2, H, BODIES, BODIES), jnp.float32), -6.0, 6.0)
    off_values = (raw_values + jnp.swapaxes(raw_values, 2, 3)) * (math.sqrt(0.5) / math.sqrt(BODIES))
    diag_re = jax.random.uniform(key_re, (H, BODIES), jnp.float32, 1.0, 3.0)
    diag_im = jax.random.uniform(key_im, (H, BODIES), jnp.float32, -2.0, 2.0)
    diag_both = jnp.stack([diag_re, diag_im])[:, :, :, None]
    same_body = jnp.arange(BODIES)[:, None] == jnp.arange(BODIES)[None, :]
    return jnp.where(same_body[None, None], diag_both, off_values).astype(jnp.bfloat16)


def draw_excite(key, part):
    shape_all = (2, H, BODIES, REALS)
    body_pos = jnp.arange(BODIES, dtype=jnp.float32) / (BODIES - 1)
    harm_pos = jnp.arange(H, dtype=jnp.float32) / (H - 1)
    base_values = jnp.clip(jax.random.normal(key, shape_all, jnp.float32), -4.0, 4.0)
    rise_factor = 3.0
    factor = (rise_factor ** body_pos)[None, None, :, None] * (0.3 ** harm_pos)[None, :, None, None]
    return base_values * factor


def levels(rng, extent, pieces, least, top_value):
    loudness = 1.0
    for position, shards_of in pieces:
        heights = jax.random.uniform(jax.random.fold_in(jax.random.fold_in(rng, 6), position), (shards_of,), jnp.float32, least / len(pieces), top_value / len(pieces))
        loudness = loudness * jnp.repeat(jnp.exp(heights), extent[position] // shards_of).reshape((-1,) + (1,) * (len(extent) - 1 - position))
    return loudness


def normal_values(stream_key, shape, deviation, limit, cuts=(), kind=jnp.bfloat16):
    loudness = levels(stream_key, shape, cuts, -0.22, 0.18) if cuts else 1.0
    drawn = jax.random.normal(stream_key, shape, jnp.float32) * deviation * loudness
    return jnp.minimum(jnp.maximum(drawn, -limit), limit).astype(kind)


def setup_inputs(seed: int = 0, part: int = 0) -> dict:
    key_list = jax.random.split(jax.random.key(seed), 6)
    part_keys = jax.random.split(jax.random.fold_in(key_list[5], part), 6)
    return {
        "vel": normal_values(part_keys[0], (2, H, BODIES, REALS), 1.0, 4.0, ((1, 4), (2, 4)), jnp.float32),
        "imped": draw_imped(jax.random.fold_in(key_list[5], 71), part),
        "excite": draw_excite(jax.random.fold_in(jax.random.fold_in(key_list[5], part), 71), part),
        "quad_coef": jnp.clip(jnp.exp(math.log(3.0) - 2.3025851 * jax.random.uniform(key_list[3], (BODIES,), jnp.float32) ** levels(key_list[3], (BODIES,), ((0, 4),), -0.2, 0.2)), 0.3, 3.0),
        "coul_coef": jnp.clip(jnp.exp(math.log(3.0) - 2.3025851 * jax.random.uniform(key_list[4], (BODIES,), jnp.float32) ** levels(key_list[4], (BODIES,), ((0, 4),), -0.2, 0.2)), 0.3, 3.0),
    }


DELTA = 0.1

def wave_tables(count, first, samples):
    harmonic = jnp.arange(count, dtype=jnp.int32) + first + 1
    sample = jnp.arange(samples, dtype=jnp.int32)
    phase = sample[:, None] * harmonic[None, :] % samples
    angle = phase.astype(jnp.float32) * (2.0 * math.pi / samples)
    return (jnp.cos(angle), jnp.sin(angle))

def pto_force(signal, quad_rows, coul_rows):
    root = jnp.sqrt(signal * signal + DELTA * DELTA)
    force_time = quad_rows[None, :] * signal * root + coul_rows[None, :] * signal / root
    slope_time = quad_rows[None, :] * (root + signal * signal / root) + coul_rows[None, :] * (DELTA * DELTA) / (root * root * root)
    return (force_time, lax.optimization_barrier(jnp.mean(slope_time, axis=0)))

def reference(vel, imped, excite, quad_coef, coul_coef):
    highest = lax.Precision.HIGHEST
    vel_low = lax.optimization_barrier(vel.astype(jnp.bfloat16)).astype(jnp.float32)

    def couple(index):
        zmat = lax.dynamic_index_in_dim(imped, index, 1, keepdims=False).astype(jnp.float32)
        xvec = lax.dynamic_index_in_dim(vel_low, index, 1, keepdims=False)
        real_part = jnp.dot(zmat[0], xvec[0], precision=highest) - jnp.dot(zmat[1], xvec[1], precision=highest)
        imag_part = jnp.dot(zmat[0], xvec[1], precision=highest) + jnp.dot(zmat[1], xvec[0], precision=highest)
        return jnp.stack([real_part, imag_part])
    coupled = jnp.swapaxes(lax.map(couple, jnp.arange(H, dtype=jnp.int32)), 0, 1)
    row_count = BODIES * REALS
    flat_rows = vel.reshape(2, H, row_count)
    cosine, sine = wave_tables(H, 0, NT)
    signal = (jnp.dot(cosine, flat_rows[0], precision=highest) - jnp.dot(sine, flat_rows[1], precision=highest)) * (1.0 / math.sqrt(H))
    quad_rows = jnp.repeat(quad_coef, REALS)
    coul_rows = jnp.repeat(coul_coef, REALS)
    force_time, mean_slope = pto_force(signal, quad_rows, coul_rows)
    scale_out = 2.0 * math.sqrt(H) / NT
    force_re = (jnp.dot(cosine.T, force_time, precision=highest) * scale_out).reshape(H, BODIES, REALS)
    force_im = (-jnp.dot(sine.T, force_time, precision=highest) * scale_out).reshape(H, BODIES, REALS)
    res_re = coupled[0] + force_re - excite[0]
    res_im = coupled[1] + force_im - excite[1]
    diag = jnp.diagonal(imped, axis1=2, axis2=3).astype(jnp.float32)
    den_re = diag[0][:, :, None] + mean_slope.reshape(BODIES, REALS)[None, :, :]
    den_im = jnp.broadcast_to(diag[1][:, :, None], den_re.shape)
    modulus = den_re * den_re + den_im * den_im
    new_re = vel[0] - (res_re * den_re + res_im * den_im) / modulus
    new_im = vel[1] - (res_im * den_re - res_re * den_im) / modulus
    total = jnp.sum(res_re * res_re) + jnp.sum(res_im * res_im)
    rms = jnp.sqrt(total / (2.0 * H * BODIES * REALS)).reshape(1)
    return (jnp.stack([new_re, new_im]), rms)
```

```python
import functools
import math

import ml_dtypes
import numpy as np
import jax
import jax.numpy as jnp
from jax import lax
from jax.experimental import pallas as pl
from jax.experimental.pallas import tpu as pltpu
from jax.sharding import PartitionSpec as P

H = 128
NT = 512
DELTA = 0.1
F32 = jnp.float32
BF16 = jnp.bfloat16


def split(x):
    high = x.astype(BF16)
    return high, (x - high.astype(F32)).astype(BF16)


def wave_constants(groups):
    k = np.arange(1, H + 1)
    phase = np.arange(NT)[None, :] * k[:, None] % NT
    angle = phase * (2.0 * math.pi / NT)
    per = H // groups
    waves = np.stack([np.cos(angle), -np.sin(angle)]).reshape(2, groups, per, NT)
    table = np.swapaxes(waves, 0, 1).reshape(2 * H, NT) / math.sqrt(H)
    table = table.astype(np.float32)
    high = table.astype(ml_dtypes.bfloat16)
    low = (table - high.astype(np.float32)).astype(ml_dtypes.bfloat16)
    forward = np.concatenate([high.T, low.T], axis=0)
    size = 2 * per
    inverse = np.stack([high.reshape(groups, size, NT), low.reshape(groups, size, NT)], axis=1).reshape(4 * H, NT)
    return forward, inverse


def pack_couple(harm, bodies, reals, vel_ref, out_ref):
    for h in range(harm):
        rows = pl.ds(h * bodies, bodies)
        re = vel_ref[rows, :]
        im = vel_ref[pl.ds((harm + h) * bodies, bodies), :]
        out_ref[rows, :] = jnp.concatenate([re, im], axis=1).astype(BF16)


def pack_time(harm, bodies, reals, vel_ref, full_ref, low_ref):
    half = bodies // 2
    for j in range(half):
        one = vel_ref[pl.ds(j, 2 * harm, stride=bodies), :]
        two = vel_ref[pl.ds(j + half, 2 * harm, stride=bodies), :]
        both = jnp.concatenate([one, two], axis=1)
        cols = pl.ds(j * 2 * reals, 2 * reals)
        full_ref[:, cols] = both
        low_ref[:, cols] = both.astype(BF16)


def time_kernel(harm, bodies, reals, quad_ref, coul_ref, own_ref, core_ref, far_ref, far_core_ref, fwd_ref, inv_ref,
                force_ref, slope_ref, high_ref, low_ref):
    step = pl.program_id(0)
    me = lax.axis_index("harm")
    size = 2 * harm
    width = own_ref.shape[1]
    group = 2 * reals
    half = bodies // 2

    def rows(index):
        return pl.ds(pl.multiple_of(index * size, size), size)

    low_ref[...] = jnp.zeros_like(low_ref)
    for ref, flip in ((own_ref, 0), (core_ref, 1)):
        high, low = split(ref[...])
        high_ref[rows(me ^ flip), :] = high
        low_ref[rows(me ^ flip), :] = low
    high_ref[rows(me ^ 2), :] = far_ref[...]
    high_ref[rows(me ^ 3), :] = far_core_ref[...]

    high = high_ref[...]
    both = jnp.dot(fwd_ref[...], high, preferred_element_type=F32)
    signal = both[:NT] + both[NT:] + jnp.dot(fwd_ref[:NT, :], low_ref[...], preferred_element_type=F32)

    lane = lax.broadcasted_iota(jnp.int32, (1, group), 1)
    quads, couls = [], []
    for g in range(width // group):
        first = step * (width // group) + g
        quads.append(jnp.where(lane < reals, quad_ref[first], quad_ref[first + half]))
        couls.append(jnp.where(lane < reals, coul_ref[first], coul_ref[first + half]))
    quad = jnp.concatenate(quads, axis=1)
    coul = jnp.concatenate(couls, axis=1)

    square = signal * signal + DELTA * DELTA
    inverse = lax.rsqrt(square)
    force_time = signal * inverse * (quad * square + coul)
    slope = inverse * ((2.0 * quad) * square - (DELTA * DELTA) * quad + (DELTA * DELTA) * coul * (inverse * inverse))
    mean = jnp.sum(slope, axis=0, keepdims=True) * (1.0 / NT)

    high, low = split(force_time)
    table = inv_ref[pl.ds(pl.multiple_of(me * 2 * size, 2 * size), 2 * size), :]
    back = jnp.dot(table, high, preferred_element_type=F32)
    back = back[:size] + back[size:] + jnp.dot(table[:size], low, preferred_element_type=F32)
    back = back * (2.0 * H / NT)

    for g in range(width // group):
        first = step * (width // group) + g
        re = back[:harm, g * group:(g + 1) * group]
        im = back[harm:, g * group:(g + 1) * group]
        force_ref[pl.ds(first, harm, stride=bodies), :] = jnp.concatenate([re[:, :reals], im[:, :reals]], axis=1)
        force_ref[pl.ds(first + half, harm, stride=bodies), :] = jnp.concatenate([re[:, reals:], im[:, reals:]], axis=1)
        part = mean[:, g * group:(g + 1) * group]
        slope_ref[pl.ds(first, 1), :] = jnp.concatenate([part[:, :reals], part[:, :reals]], axis=1)
        slope_ref[pl.ds(first + half, 1), :] = jnp.concatenate([part[:, reals:], part[:, reals:]], axis=1)


def prepare_kernel(bodies, reals, imped_ref, force_ref, slope_ref, exre_ref, exim_ref, vre_ref, vim_ref,
                   rest_ref, p_ref, q_ref, vel_ref):
    count = imped_ref.shape[1]
    everyone = imped_ref.shape[3]
    first = lax.axis_index("body") * bodies
    row = lax.broadcasted_iota(jnp.int32, (bodies, everyone), 0)
    col = lax.broadcasted_iota(jnp.int32, (bodies, everyone), 1)
    mine = col == row + first
    ones = jnp.ones((everyone, 2 * reals), BF16)
    sign = jnp.where(lax.broadcasted_iota(jnp.int32, (bodies, 2 * reals), 1) < reals, 1.0, -1.0)
    slope = slope_ref[...]
    for h in range(count):
        rows = pl.ds(h * bodies, bodies)
        real = jnp.where(mine, imped_ref[0, h], jnp.zeros((), BF16))
        imag = jnp.where(mine, imped_ref[1, h], jnp.zeros((), BF16))
        den_re = jnp.dot(real, ones, preferred_element_type=F32) + slope
        den_im = jnp.dot(imag, ones, preferred_element_type=F32)
        inverse = 1.0 / (den_re * den_re + den_im * den_im)
        p_ref[rows, :] = den_re * inverse
        q_ref[rows, :] = den_im * inverse * sign
        rest_ref[rows, :] = force_ref[rows, :] - jnp.concatenate([exre_ref[rows, :], exim_ref[rows, :]], axis=1)
        vel_ref[rows, :] = jnp.concatenate([vre_ref[rows, :], vim_ref[rows, :]], axis=1)


def couple_kernel(bodies, reals, flips, imped_ref, *refs):
    pieces, (rest_ref, res_ref, total_ref, held_ref, sum_ref) = refs[:-5], refs[-5:]
    count = imped_ref.shape[1]
    step = pl.program_id(0)
    me = lax.axis_index("body")
    sign = jnp.where(lax.broadcasted_iota(jnp.int32, (bodies, 2 * reals), 1) < reals, -1.0, 1.0)
    total = jnp.zeros((bodies, 2 * reals), F32)
    for h in range(count):
        rows = pl.ds(h * bodies, bodies)
        if flips is None:
            vels = pieces[0][:, h].reshape(-1, 2 * reals)
        else:
            slot = h % 2
            for flip, ref in zip(flips, pieces[:-2]):
                held_ref[slot, pl.ds(pl.multiple_of((me ^ flip) * bodies, bodies), bodies), :] = ref[rows, :]
            ends = jnp.logical_or(me == 0, me == 3)
            held_ref[slot, pl.ds(pl.multiple_of((me ^ 2) * bodies, bodies), bodies), :] = jnp.where(
                ends, pieces[-2][rows, :], pieces[-1][rows, :])
            vels = held_ref[slot]
        both = imped_ref[:, h].reshape(2 * bodies, imped_ref.shape[3])
        out = jnp.dot(both, vels, preferred_element_type=F32)
        coupled = out[:bodies] + sign * pltpu.roll(out[bodies:], reals, 1)
        res = coupled + rest_ref[rows, :]
        res_ref[rows, :] = res
        total = total + res * res
    kept = jnp.sum(total.reshape(bodies // 8, 8, 2 * reals), axis=0)

    @pl.when(step == 0)
    def _():
        sum_ref[...] = kept

    @pl.when(step > 0)
    def _():
        sum_ref[...] = sum_ref[...] + kept

    @pl.when(step == pl.num_programs(0) - 1)
    def _():
        total_ref[...] = jnp.broadcast_to(jnp.sum(sum_ref[...]), total_ref.shape)


def finish_kernel(bodies, reals, res_ref, p_ref, q_ref, vel_ref, out_ref):
    res = res_ref[...]
    new = vel_ref[...] - (res * p_ref[...] + pltpu.roll(res, reals, 1) * q_ref[...])
    out_ref[0] = new[:, :reals]
    out_ref[1] = new[:, reals:]


def gather_line(x, axis):
    near = lax.ppermute(x, axis, [(0, 1), (1, 0), (2, 3), (3, 2)])
    cross = lax.ppermute(x, axis, [(1, 2), (2, 1), (0, 3), (3, 0)])
    outer = lax.ppermute(cross, axis, [(1, 0), (2, 3)])
    inner = lax.ppermute(near, axis, [(1, 2), (2, 1)])
    return x, near, cross, outer, inner


def params(mib=24):
    return pltpu.CompilerParams(vmem_limit_bytes=mib << 20)


def cost(flops, moved):
    return pl.CostEstimate(flops=flops, bytes_accessed=moved, transcendentals=0)


def make_local(mesh):
    body_count = mesh.shape["body"]

    def local(vel, imped, excite, quad_coef, coul_coef):
        _, harm, bodies, reals = vel.shape
        everyone = imped.shape[3]
        group = 2 * reals
        total_rows = harm * bodies
        columns = bodies * reals
        forward, inverse = wave_constants(H // harm)
        flat = vel.reshape(2 * total_rows, reals)
        flat_excite = excite.reshape(2 * total_rows, reals)
        dense = jax.ShapeDtypeStruct((total_rows, group), F32)

        low = pl.pallas_call(
            functools.partial(pack_couple, harm, bodies, reals),
            out_shape=jax.ShapeDtypeStruct((total_rows, group), BF16),
            compiler_params=params(),
            cost_estimate=cost(0, 3 << 20),
            name="pack_couple",
        )(flat)
        if body_count == 4:
            pieces = gather_line(low, "body")
            flips = (0, 1, 3)
        else:
            pieces = (lax.all_gather(low, "body").reshape(body_count, harm, bodies, group),)
            flips = None

        own, own_low = pl.pallas_call(
            functools.partial(pack_time, harm, bodies, reals),
            out_shape=(
                jax.ShapeDtypeStruct((2 * harm, columns), F32),
                jax.ShapeDtypeStruct((2 * harm, columns), BF16),
            ),
            compiler_params=params(),
            cost_estimate=cost(0, 4 << 20),
            name="pack_time",
        )(flat)
        far = lax.ppermute(own_low, "harm", [(i, i ^ 2) for i in range(4)])
        core = lax.ppermute(own, "harm", [(i, i ^ 1) for i in range(4)])
        far_core = lax.ppermute(far, "harm", [(i, i ^ 1) for i in range(4)])

        width = 4 * group
        tile = pl.BlockSpec((2 * harm, width), lambda i: (0, i))
        force, slope = pl.pallas_call(
            functools.partial(time_kernel, harm, bodies, reals),
            grid=(columns // width,),
            in_specs=[
                pl.BlockSpec(memory_space=pltpu.SMEM),
                pl.BlockSpec(memory_space=pltpu.SMEM),
                tile, tile, tile, tile,
                pl.BlockSpec(forward.shape, lambda i: (0, 0)),
                pl.BlockSpec(inverse.shape, lambda i: (0, 0)),
            ],
            out_specs=[
                pl.BlockSpec((total_rows, group), lambda i: (0, 0)),
                pl.BlockSpec((bodies, group), lambda i: (0, 0)),
            ],
            out_shape=(dense, jax.ShapeDtypeStruct((bodies, group), F32)),
            scratch_shapes=[pltpu.VMEM((2 * H, width), BF16), pltpu.VMEM((2 * H, width), BF16)],
            compiler_params=params(),
            cost_estimate=cost(10**10, 6 << 20),
            name="time_kernel",
        )(quad_coef, coul_coef, own, core, far, far_core, jnp.asarray(forward), jnp.asarray(inverse))

        count = 8
        steps = harm // count
        block = pl.BlockSpec((count * bodies, group), lambda i: (i, 0))
        slim = pl.BlockSpec((count * bodies, reals), lambda i: (i, 0))
        slim_im = pl.BlockSpec((count * bodies, reals), lambda i: (i + steps, 0))
        wide = pl.BlockSpec((2, count, bodies, everyone), lambda i: (0, i, 0, 0))
        rest, factor_p, factor_q, vel_dense = pl.pallas_call(
            functools.partial(prepare_kernel, bodies, reals),
            grid=(steps,),
            in_specs=[wide, block, pl.BlockSpec((bodies, group), lambda i: (0, 0)), slim, slim_im, slim, slim_im],
            out_specs=[block] * 4,
            out_shape=(dense,) * 4,
            compiler_params=params(),
            cost_estimate=cost(10**9, 12 << 20),
            name="prepare",
        )(imped, force, slope, flat_excite, flat_excite, flat, flat)

        if flips is None:
            piece_specs = [pl.BlockSpec((body_count, count, bodies, group), lambda i: (0, i, 0, 0))]
        else:
            piece_specs = [block] * len(pieces)
        res, total = pl.pallas_call(
            functools.partial(couple_kernel, bodies, reals, flips),
            grid=(steps,),
            in_specs=[wide, *piece_specs, block],
            out_specs=[block, pl.BlockSpec((8, 128), lambda i: (0, 0))],
            out_shape=(dense, jax.ShapeDtypeStruct((8, 128), F32)),
            scratch_shapes=[pltpu.VMEM((2, everyone, group), BF16), pltpu.VMEM((8, group), F32)],
            compiler_params=params(),
            cost_estimate=cost(10**9, 8 << 20),
            name="couple",
        )(imped, *pieces, rest)

        new = pl.pallas_call(
            functools.partial(finish_kernel, bodies, reals),
            grid=(steps,),
            in_specs=[block] * 4,
            out_specs=pl.BlockSpec((2, count * bodies, reals), lambda i: (0, i, 0)),
            out_shape=jax.ShapeDtypeStruct((2, total_rows, reals), F32),
            compiler_params=params(),
            cost_estimate=cost(0, 6 << 20),
            name="finish",
        )(res, factor_p, factor_q, vel_dense)

        for axis, flip in (("harm", 1), ("harm", 2)):
            total = total + lax.ppermute(total, axis, [(i, i ^ flip) for i in range(4)])
        flip = 1
        while flip < body_count:
            total = total + lax.ppermute(total, "body", [(i, i ^ flip) for i in range(body_count)])
            flip *= 2
        rms = jnp.sqrt(total[0, :1] * (1.0 / (2.0 * H * everyone * reals)))
        return new.reshape(vel.shape), rms

    return local


def solution(mesh):
    in_specs = (
        P(None, "harm", "body", "sea"),
        P(None, "harm", "body", None),
        P(None, "harm", "body", "sea"),
        P("body"),
        P("body"),
    )
    out_specs = (P(None, "harm", "body", "sea"), P("sea"))
    return jax.shard_map(make_local(mesh), mesh=mesh, in_specs=in_specs, out_specs=out_specs, check_vma=False)
```

```python
import functools
import math

import ml_dtypes
import numpy as np
import jax
import jax.numpy as jnp
from jax import lax
from jax.experimental import pallas as pl
from jax.experimental.pallas import tpu as pltpu
from jax.sharding import PartitionSpec as P

H = 128
NT = 512
DELTA = 0.1
F32 = jnp.float32
BF16 = jnp.bfloat16
VMEM = pl.BlockSpec(memory_space=pltpu.VMEM)
SMEM = pl.BlockSpec(memory_space=pltpu.SMEM)


def split(x):
    high = x.astype(BF16)
    return high, (x - high.astype(F32)).astype(BF16)


def wave_constants(groups):
    k = np.arange(1, H + 1)
    phase = np.arange(NT)[None, :] * k[:, None] % NT
    angle = phase * (2.0 * math.pi / NT)
    per = H // groups
    waves = np.stack([np.cos(angle), -np.sin(angle)]).reshape(2, groups, per, NT)
    table = np.swapaxes(waves, 0, 1).reshape(2 * H, NT) / math.sqrt(H)
    table = table.astype(np.float32)
    high = table.astype(ml_dtypes.bfloat16)
    low = (table - high.astype(np.float32)).astype(ml_dtypes.bfloat16)
    forward = np.concatenate([high.T, low.T], axis=0)
    size = 2 * per
    inverse = np.stack([high.reshape(groups, size, NT), low.reshape(groups, size, NT)], axis=1).reshape(4 * H, NT)
    return forward, inverse


def pack_couple(harm, bodies, reals, vel_ref, out_ref):
    for h in range(harm):
        rows = pl.ds(h * bodies, bodies)
        re = vel_ref[rows, :]
        im = vel_ref[pl.ds((harm + h) * bodies, bodies), :]
        out_ref[rows, :] = jnp.concatenate([re, im], axis=1).astype(BF16)


def pack_time(harm, bodies, reals, vel_ref, low_ref, own_ref, send_ref, own_low_ref, send_low_ref):
    core = lax.axis_index("harm") % 2
    half = bodies // 2
    pair = bodies // 4
    outs = ((core, own_ref, own_low_ref), (1 - core, send_ref, send_low_ref))
    for which, full, low in outs:
        for j in range(pair):
            one = vel_ref[pl.ds(which * half + j, 2 * harm, stride=bodies), :]
            two = vel_ref[pl.ds(which * half + pair + j, 2 * harm, stride=bodies), :]
            both = jnp.concatenate([one, two], axis=1)
            cols = pl.ds(j * 2 * reals, 2 * reals)
            full[:, cols] = both
            low[:, cols] = both.astype(BF16)


def time_kernel(harm, bodies, reals, quad_ref, coul_ref, own_ref, core_ref, far_ref, far_core_ref, fwd_ref, inv_ref,
                mine_ref, other_ref, high_ref, low_ref):
    step = pl.program_id(0)
    me = lax.axis_index("harm")
    size = 2 * harm
    width = own_ref.shape[1]
    group = 2 * reals
    half = bodies // 2
    pair = bodies // 4
    base = (me % 2) * half

    def rows(index):
        return pl.ds(pl.multiple_of(index * size, size), size)

    @pl.when(step == 0)
    def _():
        low_ref[...] = jnp.zeros_like(low_ref)

    for ref, flip in ((own_ref, 0), (core_ref, 1)):
        high, low = split(ref[...])
        high_ref[rows(me ^ flip), :] = high
        low_ref[rows(me ^ flip), :] = low
    high_ref[rows(me ^ 2), :] = far_ref[...]
    high_ref[rows(me ^ 3), :] = far_core_ref[...]

    both = jnp.dot(fwd_ref[...], high_ref[...], preferred_element_type=F32)
    signal = both[:NT] + both[NT:] + jnp.dot(fwd_ref[:NT, :], low_ref[...], preferred_element_type=F32)

    lane = lax.broadcasted_iota(jnp.int32, (1, group), 1)
    quads, couls = [], []
    for g in range(width // group):
        first = base + step * (width // group) + g
        quads.append(jnp.where(lane < reals, quad_ref[first], quad_ref[first + pair]))
        couls.append(jnp.where(lane < reals, coul_ref[first], coul_ref[first + pair]))
    quad = jnp.concatenate(quads, axis=1)
    coul = jnp.concatenate(couls, axis=1)

    square = signal * signal + DELTA * DELTA
    inverse = lax.rsqrt(square)
    force_time = signal * inverse * (quad * square + coul)
    slope = inverse * ((2.0 * quad) * square - (DELTA * DELTA) * quad + (DELTA * DELTA) * coul * (inverse * inverse))
    mean = jnp.sum(slope, axis=0, keepdims=True) * (1.0 / NT)

    high, low = split(force_time)
    for flip, out_ref in ((0, mine_ref), (1, other_ref)):
        table = inv_ref[pl.ds(pl.multiple_of((me ^ flip) * 2 * size, 2 * size), 2 * size), :]
        back = jnp.dot(table, high, preferred_element_type=F32)
        back = back[:size] + back[size:] + jnp.dot(table[:size], low, preferred_element_type=F32)
        back = back * (2.0 * H / NT)
        for g in range(width // group):
            first = step * (width // group) + g
            re = back[:harm, g * group:(g + 1) * group]
            im = back[harm:, g * group:(g + 1) * group]
            out_ref[pl.ds(first, harm, stride=half), :] = jnp.concatenate([re[:, :reals], im[:, :reals]], axis=1)
            out_ref[pl.ds(first + pair, harm, stride=half), :] = jnp.concatenate([re[:, reals:], im[:, reals:]], axis=1)
            part = mean[:, g * group:(g + 1) * group]
            last = harm * half + first
            out_ref[pl.ds(last, 1), :] = jnp.concatenate([part[:, :reals], part[:, :reals]], axis=1)
            out_ref[pl.ds(last + pair, 1), :] = jnp.concatenate([part[:, reals:], part[:, reals:]], axis=1)


def prepare_kernel(harm, bodies, reals, imped_ref, mine_ref, other_ref, excite_ref, velocity_ref,
                   rest_ref, p_ref, q_ref, vel_ref):
    everyone = imped_ref.shape[3]
    half = bodies // 2
    core = lax.axis_index("harm") % 2
    first = lax.axis_index("body") * bodies
    row = lax.broadcasted_iota(jnp.int32, (bodies, everyone), 0)
    col = lax.broadcasted_iota(jnp.int32, (bodies, everyone), 1)
    mine = col == row + first
    ones = jnp.ones((everyone, 2 * reals), BF16)
    sign = jnp.where(lax.broadcasted_iota(jnp.int32, (bodies, 2 * reals), 1) < reals, 1.0, -1.0)
    lower = core == 0

    def halves(at):
        one = mine_ref[pl.ds(at, half), :]
        two = other_ref[pl.ds(at, half), :]
        return jnp.concatenate([jnp.where(lower, one, two), jnp.where(lower, two, one)], axis=0)

    slope = halves(harm * half)
    for h in range(harm):
        rows = pl.ds(h * bodies, bodies)
        rows_im = pl.ds((harm + h) * bodies, bodies)
        real = jnp.where(mine, imped_ref[0, h], jnp.zeros((), BF16))
        imag = jnp.where(mine, imped_ref[1, h], jnp.zeros((), BF16))
        den = jnp.dot(jnp.concatenate([real, imag], axis=0), ones, preferred_element_type=F32)
        den_re = den[:bodies] + slope
        den_im = den[bodies:]
        inverse = 1.0 / (den_re * den_re + den_im * den_im)
        p_ref[rows, :] = den_re * inverse
        q_ref[rows, :] = den_im * inverse * sign
        rest_ref[rows, :] = halves(h * half) - jnp.concatenate([excite_ref[rows, :], excite_ref[rows_im, :]], axis=1)
        vel_ref[rows, :] = jnp.concatenate([velocity_ref[rows, :], velocity_ref[rows_im, :]], axis=1)


def couple_kernel(harm, bodies, reals, flips, imped_ref, *refs):
    pieces, (rest_ref, res_ref, total_ref, held_ref) = refs[:-4], refs[-4:]
    me = lax.axis_index("body")
    sign = jnp.where(lax.broadcasted_iota(jnp.int32, (bodies, 2 * reals), 1) < reals, -1.0, 1.0)
    total = jnp.zeros((8, 2 * reals), F32)
    ends = jnp.logical_or(me == 0, me == 3)
    for h in range(harm):
        rows = pl.ds(h * bodies, bodies)
        if flips is None:
            vels = pieces[0][:, h].reshape(-1, 2 * reals)
        else:
            slot = h % 4
            for flip, ref in zip(flips, pieces[:-2]):
                held_ref[slot, pl.ds(pl.multiple_of((me ^ flip) * bodies, bodies), bodies), :] = ref[rows, :]
            held_ref[slot, pl.ds(pl.multiple_of((me ^ 2) * bodies, bodies), bodies), :] = jnp.where(
                ends, pieces[-2][rows, :], pieces[-1][rows, :])
            vels = held_ref[slot]
        both = imped_ref[:, h].reshape(2 * bodies, imped_ref.shape[3])
        out = jnp.dot(both, vels, preferred_element_type=F32)
        res = out[:bodies] + sign * pltpu.roll(out[bodies:], reals, 1) + rest_ref[rows, :]
        res_ref[rows, :] = res
        total = total + jnp.sum((res * res).reshape(bodies // 8, 8, 2 * reals), axis=0)
    total_ref[...] = jnp.broadcast_to(jnp.sum(total), total_ref.shape)


def finish_kernel(harm, bodies, reals, res_ref, p_ref, q_ref, vel_ref, out_ref):
    rows = out_ref.shape[1]
    at = pl.ds(pl.multiple_of(pl.program_id(0) * rows, rows), rows)
    res = res_ref[at, :]
    new = vel_ref[at, :] - (res * p_ref[at, :] + pltpu.roll(res, reals, 1) * q_ref[at, :])
    out_ref[0] = new[:, :reals]
    out_ref[1] = new[:, reals:]


def rms_kernel(scale, one_ref, two_ref, out_ref):
    mean = (one_ref[...] + two_ref[...]) * scale
    out_ref[0] = jnp.sqrt(mean)[0, 0]


def gather_line(x, axis):
    near = lax.ppermute(x, axis, [(0, 1), (1, 0), (2, 3), (3, 2)])
    cross = lax.ppermute(x, axis, [(1, 2), (2, 1), (0, 3), (3, 0)])
    outer = lax.ppermute(cross, axis, [(1, 0), (2, 3)])
    inner = lax.ppermute(near, axis, [(1, 2), (2, 1)])
    return x, near, cross, outer, inner


def params(mib=24):
    return pltpu.CompilerParams(vmem_limit_bytes=mib << 20)


def cost(flops, moved):
    return pl.CostEstimate(flops=flops, bytes_accessed=moved, transcendentals=0)


def make_local(mesh):
    body_count = mesh.shape["body"]

    def local(vel, imped, excite, quad_coef, coul_coef):
        _, harm, bodies, reals = vel.shape
        everyone = imped.shape[3]
        group = 2 * reals
        total_rows = harm * bodies
        forward, inverse = wave_constants(H // harm)
        flat = vel.reshape(2 * total_rows, reals)
        flat_excite = excite.reshape(2 * total_rows, reals)
        dense = jax.ShapeDtypeStruct((total_rows, group), F32)

        low = pl.pallas_call(
            functools.partial(pack_couple, harm, bodies, reals),
            out_shape=jax.ShapeDtypeStruct((total_rows, group), BF16),
            compiler_params=params(),
            cost_estimate=cost(0, 3 << 20),
            name="pack_couple",
        )(flat)
        if body_count == 4:
            pieces = gather_line(low, "body")
            flips = (0, 1, 3)
        else:
            pieces = (lax.all_gather(low, "body").reshape(body_count, harm, bodies, group),)
            flips = None

        columns = bodies * reals // 2
        packed = jax.ShapeDtypeStruct((2 * harm, columns), F32)
        packed_low = jax.ShapeDtypeStruct((2 * harm, columns), BF16)
        own, send, own_low, send_low = pl.pallas_call(
            functools.partial(pack_time, harm, bodies, reals),
            in_specs=[VMEM, pl.BlockSpec(memory_space=pl.ANY)],
            out_shape=(packed, packed, packed_low, packed_low),
            compiler_params=params(),
            cost_estimate=cost(0, 4 << 20),
            name="pack_time",
        )(flat, low)

        def flipped(x, flip):
            return lax.ppermute(x, "harm", [(i, i ^ flip) for i in range(4)])

        far = flipped(own_low, 2)
        far_core = flipped(send_low, 3)
        core = flipped(send, 1)

        width = 4 * group
        tile = pl.BlockSpec((2 * harm, width), lambda i: (0, i))
        half_rows = (harm + 1) * bodies // 2
        half_spec = pl.BlockSpec((half_rows, group), lambda i: (0, 0))
        half_shape = jax.ShapeDtypeStruct((half_rows, group), F32)
        mine, other = pl.pallas_call(
            functools.partial(time_kernel, harm, bodies, reals),
            grid=(columns // width,),
            in_specs=[SMEM, SMEM, tile, tile, tile, tile, VMEM, VMEM],
            out_specs=[half_spec, half_spec],
            out_shape=(half_shape, half_shape),
            scratch_shapes=[pltpu.VMEM((2 * H, width), BF16), pltpu.VMEM((2 * H, width), BF16)],
            compiler_params=params(),
            cost_estimate=cost(5 * 10**9, 4 << 20),
            name="time_kernel",
        )(quad_coef, coul_coef, own, core, far, far_core, jnp.asarray(forward), jnp.asarray(inverse))
        other = flipped(other, 1)

        rest, factor_p, factor_q, vel_dense = pl.pallas_call(
            functools.partial(prepare_kernel, harm, bodies, reals),
            in_specs=[VMEM] * 5,
            out_shape=(dense,) * 4,
            compiler_params=params(),
            cost_estimate=cost(10**9, 4 << 20),
            name="prepare",
        )(imped, mine, other, flat_excite, flat)

        res, total = pl.pallas_call(
            functools.partial(couple_kernel, harm, bodies, reals, flips),
            in_specs=[VMEM] * (2 + len(pieces)),
            out_shape=(dense, jax.ShapeDtypeStruct((8, 128), F32)),
            scratch_shapes=[pltpu.VMEM((4, everyone, group), BF16)],
            compiler_params=params(),
            cost_estimate=cost(10**9, 4 << 20),
            name="couple",
        )(imped, *pieces, rest)

        steps = 8
        rows = total_rows // steps
        new = pl.pallas_call(
            functools.partial(finish_kernel, harm, bodies, reals),
            grid=(steps,),
            in_specs=[VMEM] * 4,
            out_specs=pl.BlockSpec((2, rows, reals), lambda i: (0, i, 0)),
            out_shape=jax.ShapeDtypeStruct((2, total_rows, reals), F32),
            compiler_params=params(),
            cost_estimate=cost(0, 6 << 20),
            name="finish",
        )(res, factor_p, factor_q, vel_dense)

        got = flipped(total, 1)
        total = total + got
        got = flipped(total, 2)
        flip = 1
        while flip < body_count:
            total = total + got
            got = lax.ppermute(total, "body", [(i, i ^ flip) for i in range(body_count)])
            flip *= 2
        rms = pl.pallas_call(
            functools.partial(rms_kernel, 1.0 / (2.0 * H * everyone * reals)),
            in_specs=[VMEM] * 2,
            out_specs=SMEM,
            out_shape=jax.ShapeDtypeStruct((1,), F32),
            name="rms",
        )(total, got)
        return new.reshape(vel.shape), rms

    return local


def solution(mesh):
    in_specs = (
        P(None, "harm", "body", "sea"),
        P(None, "harm", "body", None),
        P(None, "harm", "body", "sea"),
        P("body"),
        P("body"),
    )
    out_specs = (P(None, "harm", "body", "sea"), P("sea"))
    return jax.shard_map(make_local(mesh), mesh=mesh, in_specs=in_specs, out_specs=out_specs, check_vma=False)
```

```python
import functools
import math

import ml_dtypes
import numpy as np
import jax
import jax.numpy as jnp
from jax import lax
from jax.experimental import pallas as pl
from jax.experimental.pallas import tpu as pltpu
from jax.sharding import PartitionSpec as P

H = 128
NT = 512
DELTA = 0.1
F32 = jnp.float32
BF16 = jnp.bfloat16
VMEM = pl.BlockSpec(memory_space=pltpu.VMEM)
SMEM = pl.BlockSpec(memory_space=pltpu.SMEM)


def split(x):
    high = x.astype(BF16)
    return high, (x - high.astype(F32)).astype(BF16)


def wave_constants(groups):
    k = np.arange(1, H + 1)
    phase = np.arange(NT)[None, :] * k[:, None] % NT
    angle = phase * (2.0 * math.pi / NT)
    waves = np.stack([np.cos(angle), -np.sin(angle)]).reshape(2, groups, H // groups, NT)
    table = (np.swapaxes(waves, 0, 1).reshape(2 * H, NT) / math.sqrt(H)).astype(np.float32)
    high = table.astype(ml_dtypes.bfloat16)
    low = (table - high.astype(np.float32)).astype(ml_dtypes.bfloat16)
    return np.concatenate([high.T, low.T], axis=1), np.concatenate([high, low, high], axis=1)


def pack_couple(harm, bodies, reals, vel_ref, out_ref):
    for h in range(harm):
        rows = pl.ds(h * bodies, bodies)
        re = vel_ref[rows, :]
        im = vel_ref[pl.ds((harm + h) * bodies, bodies), :]
        out_ref[rows, :] = jnp.concatenate([re, im], axis=1).astype(BF16)


def pack_time(harm, bodies, reals, vel_ref, own_ref, send_ref):
    core = lax.axis_index("harm") % 2
    half = bodies // 2
    pair = bodies // 4
    for which, out_ref in ((core, own_ref), (1 - core, send_ref)):
        for j in range(pair):
            one = vel_ref[pl.ds(which * half + j, 2 * harm, stride=bodies), :]
            two = vel_ref[pl.ds(which * half + pair + j, 2 * harm, stride=bodies), :]
            out_ref[:, pl.ds(j * 2 * reals, 2 * reals)] = jnp.concatenate([one, two], axis=1).astype(BF16)


def time_kernel(harm, bodies, reals, quad_ref, coul_ref, own_ref, core_ref, far_ref, far_core_ref, fwd_ref, inv_ref,
                mine_ref, other_ref, held_ref, force_ref):
    step = pl.program_id(0)
    me = lax.axis_index("harm")
    core = me % 2
    size = 2 * harm
    width = own_ref.shape[1]
    group = 2 * reals
    pair = bodies // 4
    base = core * (bodies // 2) + step * (width // group)
    small = DELTA * DELTA

    for flip, ref in enumerate((own_ref, core_ref, far_ref, far_core_ref)):
        value = ref[...]
        first = pl.multiple_of((me ^ flip) * size, size)
        held_ref[pl.ds(first, size), :] = value
        held_ref[pl.ds(first + 2 * H, size), :] = value

    lane = lax.broadcasted_iota(jnp.int32, (1, group), 1)
    quads, couls = [], []
    for g in range(width // group):
        quads.append(jnp.where(lane < reals, quad_ref[base + g], quad_ref[base + g + pair]))
        couls.append(jnp.where(lane < reals, coul_ref[base + g], coul_ref[base + g + pair]))
    quad = jnp.concatenate(quads, axis=1)
    coul = jnp.concatenate(couls, axis=1)

    signal = jnp.dot(fwd_ref[...], held_ref[...], preferred_element_type=F32)
    square = signal * signal + small
    inverse = lax.rsqrt(square)
    root = square * inverse
    high, low = split(signal * (quad * root + coul * inverse))
    force_ref[:NT] = high
    force_ref[NT:2 * NT] = high
    force_ref[2 * NT:] = low
    roots = jnp.sum(root, axis=0, keepdims=True)
    inverses = jnp.sum(inverse, axis=0, keepdims=True)
    cubes = jnp.sum(inverse * inverse * inverse, axis=0, keepdims=True)
    mean = (quad * (2.0 * roots - small * inverses) + coul * (small * cubes)) * (1.0 / NT)

    first = pl.multiple_of((me // 2) * 2 * size, 2 * size)
    back = jnp.dot(inv_ref[pl.ds(first, 2 * size), :], force_ref[...], preferred_element_type=F32) * (2.0 * H / NT)
    lower = core == 0
    mine_ref[:size] = jnp.where(lower, back[:size], back[size:])
    other_ref[:size] = jnp.where(lower, back[size:], back[:size])
    slope = jnp.broadcast_to(mean, (8, width))
    mine_ref[size:] = slope
    other_ref[size:] = slope


def prepare_kernel(harm, bodies, reals, imped_ref, mine_ref, other_ref, excite_ref, velocity_ref,
                   rest_ref, p_ref, q_ref, vel_ref, slope_ref):
    everyone = imped_ref.shape[3]
    group = 2 * reals
    half = bodies // 2
    pair = bodies // 4
    core = lax.axis_index("harm") % 2
    for which, ref in ((core, mine_ref), (1 - core, other_ref)):
        for j in range(pair):
            cols = slice(j * group, (j + 1) * group)
            re = ref[:harm, cols]
            im = ref[harm:2 * harm, cols]
            slope = ref[2 * harm:2 * harm + 1, cols]
            one = which * half + j
            two = one + pair
            rest_ref[pl.ds(one, harm, stride=bodies), :] = jnp.concatenate([re[:, :reals], im[:, :reals]], axis=1)
            rest_ref[pl.ds(two, harm, stride=bodies), :] = jnp.concatenate([re[:, reals:], im[:, reals:]], axis=1)
            slope_ref[pl.ds(one, 1), :] = jnp.concatenate([slope[:, :reals], slope[:, :reals]], axis=1)
            slope_ref[pl.ds(two, 1), :] = jnp.concatenate([slope[:, reals:], slope[:, reals:]], axis=1)

    first = lax.axis_index("body") * bodies
    row = lax.broadcasted_iota(jnp.int32, (bodies, everyone), 0)
    col = lax.broadcasted_iota(jnp.int32, (bodies, everyone), 1)
    mine = col == row + first
    ones = jnp.ones((everyone, group), BF16)
    sign = jnp.where(lax.broadcasted_iota(jnp.int32, (bodies, group), 1) < reals, 1.0, -1.0)
    slope = slope_ref[...]
    for h in range(harm):
        rows = pl.ds(h * bodies, bodies)
        rows_im = pl.ds((harm + h) * bodies, bodies)
        real = jnp.where(mine, imped_ref[0, h], jnp.zeros((), BF16))
        imag = jnp.where(mine, imped_ref[1, h], jnp.zeros((), BF16))
        den = jnp.dot(jnp.concatenate([real, imag], axis=0), ones, preferred_element_type=F32)
        den_re = den[:bodies] + slope
        den_im = den[bodies:]
        inverse = 1.0 / (den_re * den_re + den_im * den_im)
        p_ref[rows, :] = den_re * inverse
        q_ref[rows, :] = den_im * inverse * sign
        vel = jnp.concatenate([velocity_ref[rows, :], velocity_ref[rows_im, :]], axis=1)
        vel_ref[rows, :] = vel
        excite = jnp.concatenate([excite_ref[rows, :], excite_ref[rows_im, :]], axis=1)
        rest_ref[rows, :] = rest_ref[rows, :] - excite + slope * (vel - vel.astype(BF16).astype(F32))


def couple_kernel(harm, bodies, reals, flips, imped_ref, *refs):
    pieces, (rest_ref, res_ref, total_ref, held_ref) = refs[:-4], refs[-4:]
    me = lax.axis_index("body")
    sign = jnp.where(lax.broadcasted_iota(jnp.int32, (bodies, 2 * reals), 1) < reals, -1.0, 1.0)
    total = jnp.zeros((8, 2 * reals), F32)
    ends = jnp.logical_or(me == 0, me == 3)
    for h in range(harm):
        rows = pl.ds(h * bodies, bodies)
        if flips is None:
            vels = pieces[0][:, h].reshape(-1, 2 * reals)
        else:
            slot = h % 4
            for flip, ref in zip(flips, pieces[:-2]):
                held_ref[slot, pl.ds(pl.multiple_of((me ^ flip) * bodies, bodies), bodies), :] = ref[rows, :]
            held_ref[slot, pl.ds(pl.multiple_of((me ^ 2) * bodies, bodies), bodies), :] = jnp.where(
                ends, pieces[-1][rows, :], pieces[-2][rows, :])
            vels = held_ref[slot]
        both = imped_ref[:, h].reshape(2 * bodies, imped_ref.shape[3])
        out = jnp.dot(both, vels, preferred_element_type=F32)
        res = out[:bodies] + sign * pltpu.roll(out[bodies:], reals, 1) + rest_ref[rows, :]
        res_ref[rows, :] = res
        total = total + jnp.sum((res * res).reshape(bodies // 8, 8, 2 * reals), axis=0)
    total_ref[...] = jnp.broadcast_to(jnp.sum(total), total_ref.shape)


def finish_kernel(harm, bodies, reals, res_ref, p_ref, q_ref, vel_ref, out_ref):
    rows = out_ref.shape[1]
    at = pl.ds(pl.multiple_of(pl.program_id(0) * rows, rows), rows)
    res = res_ref[at, :]
    new = vel_ref[at, :] - (res * p_ref[at, :] + pltpu.roll(res, reals, 1) * q_ref[at, :])
    out_ref[0] = new[:, :reals]
    out_ref[1] = new[:, reals:]


def rms_kernel(scale, one_ref, two_ref, out_ref):
    mean = (one_ref[...] + two_ref[...]) * scale
    out_ref[0] = jnp.sqrt(mean)[0, 0]


def gather_line(x, axis):
    near = lax.ppermute(x, axis, [(0, 1), (1, 0), (2, 3), (3, 2)])
    cross = lax.ppermute(x, axis, [(1, 2), (2, 1), (0, 3), (3, 0)])
    inner = lax.ppermute(near, axis, [(1, 2), (2, 1)])
    outer = lax.ppermute(cross, axis, [(1, 0), (2, 3)])
    return x, near, cross, inner, outer


def params(mib=24):
    return pltpu.CompilerParams(vmem_limit_bytes=mib << 20)


def cost(flops, moved):
    return pl.CostEstimate(flops=flops, bytes_accessed=moved, transcendentals=0)


def make_local(mesh):
    body_count = mesh.shape["body"]

    def local(vel, imped, excite, quad_coef, coul_coef):
        _, harm, bodies, reals = vel.shape
        everyone = imped.shape[3]
        group = 2 * reals
        total_rows = harm * bodies
        forward, inverse = wave_constants(H // harm)
        flat = vel.reshape(2 * total_rows, reals)
        flat_excite = excite.reshape(2 * total_rows, reals)
        dense = jax.ShapeDtypeStruct((total_rows, group), F32)

        def flipped(x, flip):
            return lax.ppermute(x, "harm", [(i, i ^ flip) for i in range(4)])

        low = pl.pallas_call(
            functools.partial(pack_couple, harm, bodies, reals),
            out_shape=jax.ShapeDtypeStruct((total_rows, group), BF16),
            compiler_params=params(),
            cost_estimate=cost(0, 1 << 10),
            name="pack_couple",
        )(flat)
        if body_count == 4:
            pieces = gather_line(low, "body")
            flips = (0, 1, 3)
        else:
            pieces = (lax.all_gather(low, "body").reshape(body_count, harm, bodies, group),)
            flips = None

        columns = bodies * reals // 2
        own, send = pl.pallas_call(
            functools.partial(pack_time, harm, bodies, reals),
            in_specs=[VMEM],
            out_shape=(jax.ShapeDtypeStruct((2 * harm, columns), BF16),) * 2,
            compiler_params=params(),
            cost_estimate=cost(0, 1 << 10),
            name="pack_time",
        )(flat)
        far = flipped(own, 2)
        far_core = flipped(send, 3)
        core = flipped(send, 1)

        width = 8 * group
        tile = pl.BlockSpec((2 * harm, width), lambda i: (0, i))
        half_spec = pl.BlockSpec((2 * harm + 8, width), lambda i: (0, i))
        half_shape = jax.ShapeDtypeStruct((2 * harm + 8, columns), F32)
        mine, other = pl.pallas_call(
            functools.partial(time_kernel, harm, bodies, reals),
            grid=(columns // width,),
            in_specs=[SMEM, SMEM, tile, tile, tile, tile, VMEM, VMEM],
            out_specs=[half_spec, half_spec],
            out_shape=(half_shape, half_shape),
            scratch_shapes=[pltpu.VMEM((4 * H, width), BF16), pltpu.VMEM((3 * NT, width), BF16)],
            compiler_params=params(),
            cost_estimate=cost(0, 1 << 10),
            name="time_kernel",
        )(quad_coef, coul_coef, own, core, far, far_core, jnp.asarray(forward), jnp.asarray(inverse))
        other = flipped(other, 1)

        rest, factor_p, factor_q, vel_dense = pl.pallas_call(
            functools.partial(prepare_kernel, harm, bodies, reals),
            in_specs=[VMEM] * 5,
            out_shape=(dense,) * 4,
            scratch_shapes=[pltpu.VMEM((bodies, group), F32)],
            compiler_params=params(),
            cost_estimate=cost(0, 1 << 10),
            name="prepare",
        )(imped, mine, other, flat_excite, flat)

        res, total = pl.pallas_call(
            functools.partial(couple_kernel, harm, bodies, reals, flips),
            in_specs=[VMEM] * (2 + len(pieces)),
            out_shape=(dense, jax.ShapeDtypeStruct((8, 128), F32)),
            scratch_shapes=[pltpu.VMEM((4, everyone, group), BF16)],
            compiler_params=params(),
            cost_estimate=cost(0, 1 << 10),
            name="couple",
        )(imped, *pieces, rest)

        steps = 2
        rows = total_rows // steps
        new = pl.pallas_call(
            functools.partial(finish_kernel, harm, bodies, reals),
            grid=(steps,),
            in_specs=[VMEM] * 4,
            out_specs=pl.BlockSpec((2, rows, reals), lambda i: (0, i, 0)),
            out_shape=jax.ShapeDtypeStruct((2, total_rows, reals), F32),
            compiler_params=params(),
            cost_estimate=cost(0, 1 << 10),
            name="finish",
        )(res, factor_p, factor_q, vel_dense)

        got = flipped(total, 1)
        total = total + got
        got = flipped(total, 2)
        flip = 1
        while flip < body_count:
            total = total + got
            got = lax.ppermute(total, "body", [(i, i ^ flip) for i in range(body_count)])
            flip *= 2
        rms = pl.pallas_call(
            functools.partial(rms_kernel, 1.0 / (2.0 * H * everyone * reals)),
            in_specs=[VMEM] * 2,
            out_specs=SMEM,
            out_shape=jax.ShapeDtypeStruct((1,), F32),
            compiler_params=params(),
            name="rms",
        )(total, got)
        return new.reshape(vel.shape), rms

    return local


def solution(mesh):
    in_specs = (
        P(None, "harm", "body", "sea"),
        P(None, "harm", "body", None),
        P(None, "harm", "body", "sea"),
        P("body"),
        P("body"),
    )
    out_specs = (P(None, "harm", "body", "sea"), P("sea"))
    return jax.shard_map(make_local(mesh), mesh=mesh, in_specs=in_specs, out_specs=out_specs, check_vma=False)
```

```python
import functools
import math

import ml_dtypes
import numpy as np
import jax
import jax.numpy as jnp
from jax import lax
from jax.experimental import pallas as pl
from jax.experimental.pallas import tpu as pltpu
from jax.sharding import PartitionSpec as P

H = 128
NT = 512
DELTA = 0.1
F32 = jnp.float32
BF16 = jnp.bfloat16
VMEM = pl.BlockSpec(memory_space=pltpu.VMEM)
SMEM = pl.BlockSpec(memory_space=pltpu.SMEM)


def split(x):
    high = x.astype(BF16)
    return high, (x - high.astype(F32)).astype(BF16)


def wave_constants(groups):
    k = np.arange(1, H + 1)
    phase = np.arange(NT)[None, :] * k[:, None] % NT
    angle = phase * (2.0 * math.pi / NT)
    waves = np.stack([np.cos(angle), -np.sin(angle)]).reshape(2, groups, H // groups, NT)
    table = (np.swapaxes(waves, 0, 1).reshape(2 * H, NT) / math.sqrt(H)).astype(np.float32)
    high = table.astype(ml_dtypes.bfloat16)
    low = (table - high.astype(np.float32)).astype(ml_dtypes.bfloat16)
    return np.concatenate([high.T, low.T], axis=1), np.concatenate([high, low, high], axis=1)


def pack_couple(harm, bodies, reals, vel_ref, out_ref):
    for h in range(harm):
        rows = pl.ds(h * bodies, bodies)
        re = vel_ref[rows, :]
        im = vel_ref[pl.ds((harm + h) * bodies, bodies), :]
        out_ref[rows, :] = jnp.concatenate([re, im], axis=1).astype(BF16)


def pack_time(harm, bodies, reals, vel_ref, own_ref, send_ref, again_ref):
    core = lax.axis_index("harm") % 2
    half = bodies // 2
    pair = bodies // 4
    for which, out_ref in ((core, own_ref), (1 - core, send_ref)):
        for j in range(pair):
            one = vel_ref[pl.ds(which * half + j, 2 * harm, stride=bodies), :]
            two = vel_ref[pl.ds(which * half + pair + j, 2 * harm, stride=bodies), :]
            out_ref[:, pl.ds(j * 2 * reals, 2 * reals)] = jnp.concatenate([one, two], axis=1).astype(BF16)
    pack_couple(harm, bodies, reals, vel_ref, again_ref)


def time_kernel(harm, bodies, reals, quad_ref, coul_ref, own_ref, core_ref, far_ref, far_core_ref, fwd_ref, inv_ref,
                mine_ref, other_ref, other_im_ref, held_ref, force_ref):
    step = pl.program_id(0)
    me = lax.axis_index("harm")
    core = me % 2
    size = 2 * harm
    width = own_ref.shape[1]
    group = 2 * reals
    pair = bodies // 4
    base = core * (bodies // 2) + step * (width // group)
    small = DELTA * DELTA

    for flip, ref in enumerate((own_ref, core_ref, far_ref, far_core_ref)):
        value = ref[...]
        first = pl.multiple_of((me ^ flip) * size, size)
        held_ref[pl.ds(first, size), :] = value
        held_ref[pl.ds(first + 2 * H, size), :] = value

    lane = lax.broadcasted_iota(jnp.int32, (1, group), 1)
    quads, couls = [], []
    for g in range(width // group):
        quads.append(jnp.where(lane < reals, quad_ref[base + g], quad_ref[base + g + pair]))
        couls.append(jnp.where(lane < reals, coul_ref[base + g], coul_ref[base + g + pair]))
    quad = jnp.concatenate(quads, axis=1)
    coul = jnp.concatenate(couls, axis=1)

    signal = jnp.dot(fwd_ref[...], held_ref[...], preferred_element_type=F32)
    square = signal * signal + small
    inverse = lax.rsqrt(square)
    root = square * inverse
    high, low = split(signal * (quad * root + coul * inverse))
    force_ref[:NT] = high
    force_ref[NT:2 * NT] = high
    force_ref[2 * NT:] = low
    roots = jnp.sum(root, axis=0, keepdims=True)
    inverses = jnp.sum(inverse, axis=0, keepdims=True)
    cubes = jnp.sum(inverse * inverse * inverse, axis=0, keepdims=True)
    mean = (quad * (2.0 * roots - small * inverses) + coul * (small * cubes)) * (1.0 / NT)

    first = pl.multiple_of((me // 2) * 2 * size, 2 * size)
    back = jnp.dot(inv_ref[pl.ds(first, 2 * size), :], force_ref[...], preferred_element_type=F32) * (2.0 * H / NT)
    lower = core == 0
    mine_ref[:size] = jnp.where(lower, back[:size], back[size:])
    other = jnp.where(lower, back[size:], back[:size])
    slope = jnp.broadcast_to(mean, (8, width))
    mine_ref[size:] = slope
    other_ref[...] = other[:harm]
    other_im_ref[:harm] = other[harm:]
    other_im_ref[harm:] = slope


def prepare_kernel(harm, bodies, reals, imped_ref, mine_ref, other_re_ref, other_im_ref, excite_ref, velocity_ref,
                   rest_ref, p_ref, q_ref, vel_ref, slope_ref):
    everyone = imped_ref.shape[3]
    group = 2 * reals
    half = bodies // 2
    pair = bodies // 4
    core = lax.axis_index("harm") % 2
    mine_re_ref, mine_im_ref = mine_ref.at[:harm], mine_ref.at[harm:]
    for which, re_ref, im_ref in ((core, mine_re_ref, mine_im_ref), (1 - core, other_re_ref, other_im_ref)):
        for j in range(pair):
            cols = slice(j * group, (j + 1) * group)
            re = re_ref[:, cols]
            im = im_ref[:harm, cols]
            slope = im_ref[harm:harm + 1, cols]
            one = which * half + j
            two = one + pair
            rest_ref[pl.ds(one, harm, stride=bodies), :] = jnp.concatenate([re[:, :reals], im[:, :reals]], axis=1)
            rest_ref[pl.ds(two, harm, stride=bodies), :] = jnp.concatenate([re[:, reals:], im[:, reals:]], axis=1)
            slope_ref[pl.ds(one, 1), :] = jnp.concatenate([slope[:, :reals], slope[:, :reals]], axis=1)
            slope_ref[pl.ds(two, 1), :] = jnp.concatenate([slope[:, reals:], slope[:, reals:]], axis=1)

    first = lax.axis_index("body") * bodies
    row = lax.broadcasted_iota(jnp.int32, (bodies, everyone), 0)
    col = lax.broadcasted_iota(jnp.int32, (bodies, everyone), 1)
    mine = col == row + first
    ones = jnp.ones((everyone, group), BF16)
    sign = jnp.where(lax.broadcasted_iota(jnp.int32, (bodies, group), 1) < reals, 1.0, -1.0)
    slope = slope_ref[...]
    for h in range(harm):
        rows = pl.ds(h * bodies, bodies)
        rows_im = pl.ds((harm + h) * bodies, bodies)
        real = jnp.where(mine, imped_ref[0, h], jnp.zeros((), BF16))
        imag = jnp.where(mine, imped_ref[1, h], jnp.zeros((), BF16))
        den = jnp.dot(jnp.concatenate([real, imag], axis=0), ones, preferred_element_type=F32)
        den_re = den[:bodies] + slope
        den_im = den[bodies:]
        inverse = 1.0 / (den_re * den_re + den_im * den_im)
        p_ref[rows, :] = den_re * inverse
        q_ref[rows, :] = den_im * inverse * sign
        vel = jnp.concatenate([velocity_ref[rows, :], velocity_ref[rows_im, :]], axis=1)
        vel_ref[rows, :] = vel
        excite = jnp.concatenate([excite_ref[rows, :], excite_ref[rows_im, :]], axis=1)
        rest_ref[rows, :] = rest_ref[rows, :] - excite + slope * (vel - vel.astype(BF16).astype(F32))


def couple_kernel(harm, bodies, reals, line, imped_ref, *refs):
    pieces, (rest_ref, res_ref, total_ref, held_ref) = refs[:-4], refs[-4:]
    me = lax.axis_index("body")
    sign = jnp.where(lax.broadcasted_iota(jnp.int32, (bodies, 2 * reals), 1) < reals, -1.0, 1.0)
    total = jnp.zeros((8, 2 * reals), F32)
    ends = jnp.logical_or(me == 0, me == 3)
    for h in range(harm):
        rows = pl.ds(h * bodies, bodies)
        if not line:
            vels = pieces[0][:, h].reshape(-1, 2 * reals)
        else:
            slot = h % 4
            held = [ref[rows, :] for ref in pieces]
            for flip, value in ((0, held[0]), (1, held[1]), (3, jnp.where(ends, held[3], held[2])),
                                (2, jnp.where(ends, held[4], held[5]))):
                held_ref[slot, pl.ds(pl.multiple_of((me ^ flip) * bodies, bodies), bodies), :] = value
            vels = held_ref[slot]
        both = imped_ref[:, h].reshape(2 * bodies, imped_ref.shape[3])
        out = jnp.dot(both, vels, preferred_element_type=F32)
        res = out[:bodies] + sign * pltpu.roll(out[bodies:], reals, 1) + rest_ref[rows, :]
        res_ref[rows, :] = res
        total = total + jnp.sum((res * res).reshape(bodies // 8, 8, 2 * reals), axis=0)
    total_ref[...] = jnp.broadcast_to(jnp.sum(total), total_ref.shape)


def finish_kernel(harm, bodies, reals, res_ref, p_ref, q_ref, vel_ref, out_ref):
    rows = out_ref.shape[1]
    at = pl.ds(pl.multiple_of(pl.program_id(0) * rows, rows), rows)
    res = res_ref[at, :]
    new = vel_ref[at, :] - (res * p_ref[at, :] + pltpu.roll(res, reals, 1) * q_ref[at, :])
    out_ref[0] = new[:, :reals]
    out_ref[1] = new[:, reals:]


def rms_kernel(scale, one_ref, two_ref, out_ref):
    mean = (one_ref[...] + two_ref[...]) * scale
    out_ref[0] = jnp.sqrt(mean)[0, 0]


def gather_line(x, again, axis):
    near = lax.ppermute(x, axis, [(0, 1), (1, 0), (2, 3), (3, 2)])
    cross = lax.ppermute(x, axis, [(1, 2), (2, 1)])
    across = lax.ppermute(again, axis, [(0, 3), (3, 0)])
    outer = lax.ppermute(cross, axis, [(1, 0), (2, 3)])
    inner = lax.ppermute(near, axis, [(1, 2), (2, 1)])
    return x, near, cross, across, outer, inner


def params(mib=24):
    return pltpu.CompilerParams(vmem_limit_bytes=mib << 20)


def cost(flops, moved):
    return pl.CostEstimate(flops=flops, bytes_accessed=moved, transcendentals=0)


def make_local(mesh):
    body_count = mesh.shape["body"]

    def local(vel, imped, excite, quad_coef, coul_coef):
        _, harm, bodies, reals = vel.shape
        everyone = imped.shape[3]
        group = 2 * reals
        total_rows = harm * bodies
        forward, inverse = wave_constants(H // harm)
        flat = vel.reshape(2 * total_rows, reals)
        flat_excite = excite.reshape(2 * total_rows, reals)
        dense = jax.ShapeDtypeStruct((total_rows, group), F32)

        def flipped(x, flip):
            return lax.ppermute(x, "harm", [(i, i ^ flip) for i in range(4)])

        low = pl.pallas_call(
            functools.partial(pack_couple, harm, bodies, reals),
            out_shape=jax.ShapeDtypeStruct((total_rows, group), BF16),
            compiler_params=params(),
            cost_estimate=cost(0, 1 << 10),
            name="pack_couple",
        )(flat)
        columns = bodies * reals // 2
        own, send, again = pl.pallas_call(
            functools.partial(pack_time, harm, bodies, reals),
            in_specs=[VMEM],
            out_shape=(
                *[jax.ShapeDtypeStruct((2 * harm, columns), BF16)] * 2,
                jax.ShapeDtypeStruct((total_rows, group), BF16),
            ),
            compiler_params=params(),
            cost_estimate=cost(0, 1 << 10),
            name="pack_time",
        )(flat)
        if body_count == 4:
            pieces = gather_line(low, again, "body")
        else:
            pieces = (lax.all_gather(low, "body").reshape(body_count, harm, bodies, group),)

        far = flipped(own, 2)
        far_core = flipped(send, 3)
        core = flipped(send, 1)

        width = 8 * group
        tile = pl.BlockSpec((2 * harm, width), lambda i: (0, i))
        heights = (2 * harm + 8, harm, harm + 8)
        mine, *other = pl.pallas_call(
            functools.partial(time_kernel, harm, bodies, reals),
            grid=(columns // width,),
            in_specs=[SMEM, SMEM, tile, tile, tile, tile, VMEM, VMEM],
            out_specs=[pl.BlockSpec((height, width), lambda i: (0, i)) for height in heights],
            out_shape=tuple(jax.ShapeDtypeStruct((height, columns), F32) for height in heights),
            scratch_shapes=[pltpu.VMEM((4 * H, width), BF16), pltpu.VMEM((3 * NT, width), BF16)],
            compiler_params=params(),
            cost_estimate=cost(0, 1 << 10),
            name="time_kernel",
        )(quad_coef, coul_coef, own, core, far, far_core, jnp.asarray(forward), jnp.asarray(inverse))
        other = [flipped(part, 1) for part in other]

        rest, factor_p, factor_q, vel_dense = pl.pallas_call(
            functools.partial(prepare_kernel, harm, bodies, reals),
            in_specs=[VMEM] * 6,
            out_shape=(dense,) * 4,
            scratch_shapes=[pltpu.VMEM((bodies, group), F32)],
            compiler_params=params(),
            cost_estimate=cost(0, 1 << 10),
            name="prepare",
        )(imped, mine, *other, flat_excite, flat)

        res, total = pl.pallas_call(
            functools.partial(couple_kernel, harm, bodies, reals, body_count == 4),
            in_specs=[VMEM] * (2 + len(pieces)),
            out_shape=(dense, jax.ShapeDtypeStruct((8, 128), F32)),
            scratch_shapes=[pltpu.VMEM((4, everyone, group), BF16)],
            compiler_params=params(),
            cost_estimate=cost(0, 1 << 10),
            name="couple",
        )(imped, *pieces, rest)

        steps = 2
        rows = total_rows // steps
        new = pl.pallas_call(
            functools.partial(finish_kernel, harm, bodies, reals),
            grid=(steps,),
            in_specs=[VMEM] * 4,
            out_specs=pl.BlockSpec((2, rows, reals), lambda i: (0, i, 0)),
            out_shape=jax.ShapeDtypeStruct((2, total_rows, reals), F32),
            compiler_params=params(),
            cost_estimate=cost(0, 1 << 10),
            name="finish",
        )(res, factor_p, factor_q, vel_dense)

        got = flipped(total, 1)
        total = total + got
        got = flipped(total, 2)
        flip = 1
        while flip < body_count:
            total = total + got
            got = lax.ppermute(total, "body", [(i, i ^ flip) for i in range(body_count)])
            flip *= 2
        rms = pl.pallas_call(
            functools.partial(rms_kernel, 1.0 / (2.0 * H * everyone * reals)),
            in_specs=[VMEM] * 2,
            out_specs=SMEM,
            out_shape=jax.ShapeDtypeStruct((1,), F32),
            compiler_params=params(),
            name="rms",
        )(total, got)
        return new.reshape(vel.shape), rms

    return local


def solution(mesh):
    in_specs = (
        P(None, "harm", "body", "sea"),
        P(None, "harm", "body", None),
        P(None, "harm", "body", "sea"),
        P("body"),
        P("body"),
    )
    out_specs = (P(None, "harm", "body", "sea"), P("sea"))
    return jax.shard_map(make_local(mesh), mesh=mesh, in_specs=in_specs, out_specs=out_specs, check_vma=False)
```

```python
import functools
import math

import ml_dtypes
import numpy as np
import jax
import jax.numpy as jnp
from jax import lax
from jax.experimental import pallas as pl
from jax.experimental.pallas import tpu as pltpu
from jax.sharding import PartitionSpec as P

H = 128
NT = 512
DELTA = 0.1
F32 = jnp.float32
BF16 = jnp.bfloat16
VMEM = pl.BlockSpec(memory_space=pltpu.VMEM)
SMEM = pl.BlockSpec(memory_space=pltpu.SMEM)


def split(x):
    high = x.astype(BF16)
    return high, (x - high.astype(F32)).astype(BF16)


def wave_constants(groups):
    k = np.arange(1, H + 1)
    phase = np.arange(NT)[None, :] * k[:, None] % NT
    angle = phase * (2.0 * math.pi / NT)
    waves = np.stack([np.cos(angle), -np.sin(angle)]).reshape(2, groups, H // groups, NT)
    table = (np.swapaxes(waves, 0, 1).reshape(2 * H, NT) / math.sqrt(H)).astype(np.float32)
    high = table.astype(ml_dtypes.bfloat16)
    low = (table - high.astype(np.float32)).astype(ml_dtypes.bfloat16)
    return np.concatenate([high.T, low.T], axis=1), np.concatenate([high, low, high], axis=1)


def pack_couple(harm, bodies, reals, vel_ref, out_ref):
    for h in range(harm):
        rows = pl.ds(h * bodies, bodies)
        re = vel_ref[rows, :]
        im = vel_ref[pl.ds((harm + h) * bodies, bodies), :]
        out_ref[rows, :] = jnp.concatenate([re, im], axis=1).astype(BF16)


def pack_time(harm, bodies, reals, vel_ref, own_ref, send_ref, again_ref):
    core = lax.axis_index("harm") % 2
    half = bodies // 2
    pair = bodies // 4
    for which, out_ref in ((core, own_ref), (1 - core, send_ref)):
        for j in range(pair):
            one = vel_ref[pl.ds(which * half + j, 2 * harm, stride=bodies), :]
            two = vel_ref[pl.ds(which * half + pair + j, 2 * harm, stride=bodies), :]
            out_ref[:, pl.ds(j * 2 * reals, 2 * reals)] = jnp.concatenate([one, two], axis=1).astype(BF16)
    pack_couple(harm, bodies, reals, vel_ref, again_ref)


def time_kernel(harm, bodies, reals, quad_ref, coul_ref, own_ref, core_ref, far_ref, far_core_ref, fwd_ref, inv_ref,
                mine_ref, other_ref, other_im_ref, held_ref, force_ref):
    step = pl.program_id(0)
    me = lax.axis_index("harm")
    core = me % 2
    size = 2 * harm
    width = own_ref.shape[1]
    group = 2 * reals
    pair = bodies // 4
    base = core * (bodies // 2) + step * (width // group)
    small = DELTA * DELTA

    for flip, ref in enumerate((own_ref, core_ref, far_ref, far_core_ref)):
        value = ref[...]
        first = pl.multiple_of((me ^ flip) * size, size)
        held_ref[pl.ds(first, size), :] = value
        held_ref[pl.ds(first + 2 * H, size), :] = value

    lane = lax.broadcasted_iota(jnp.int32, (1, group), 1)
    quads, couls = [], []
    for g in range(width // group):
        quads.append(jnp.where(lane < reals, quad_ref[base + g], quad_ref[base + g + pair]))
        couls.append(jnp.where(lane < reals, coul_ref[base + g], coul_ref[base + g + pair]))
    quad = jnp.concatenate(quads, axis=1)
    coul = jnp.concatenate(couls, axis=1)

    signal = jnp.dot(fwd_ref[...], held_ref[...], preferred_element_type=F32)
    square = signal * signal + small
    inverse = lax.rsqrt(square)
    root = square * inverse
    high, low = split(signal * (quad * root + coul * inverse))
    force_ref[:NT] = high
    force_ref[NT:2 * NT] = high
    force_ref[2 * NT:] = low
    roots = jnp.sum(root, axis=0, keepdims=True)
    inverses = jnp.sum(inverse, axis=0, keepdims=True)
    cubes = jnp.sum(inverse * inverse * inverse, axis=0, keepdims=True)
    mean = (quad * (2.0 * roots - small * inverses) + coul * (small * cubes)) * (1.0 / NT)

    first = pl.multiple_of((me // 2) * 2 * size, 2 * size)
    back = jnp.dot(inv_ref[pl.ds(first, 2 * size), :], force_ref[...], preferred_element_type=F32) * (2.0 * H / NT)
    lower = core == 0
    mine_ref[:size] = jnp.where(lower, back[:size], back[size:])
    other = jnp.where(lower, back[size:], back[:size])
    slope = jnp.broadcast_to(mean, (8, width))
    mine_ref[size:] = slope
    other_ref[...] = other[:harm]
    other_im_ref[:harm] = other[harm:]
    other_im_ref[harm:] = slope


def prepare_kernel(harm, bodies, reals, imped_ref, mine_ref, other_re_ref, other_im_ref, excite_ref, velocity_ref,
                   rest_ref, p_ref, q_ref, vel_ref, slope_ref):
    everyone = imped_ref.shape[3]
    group = 2 * reals
    half = bodies // 2
    pair = bodies // 4
    core = lax.axis_index("harm") % 2
    mine_re_ref, mine_im_ref = mine_ref.at[:harm], mine_ref.at[harm:]
    for which, re_ref, im_ref in ((core, mine_re_ref, mine_im_ref), (1 - core, other_re_ref, other_im_ref)):
        for j in range(pair):
            cols = slice(j * group, (j + 1) * group)
            re = re_ref[:, cols]
            im = im_ref[:harm, cols]
            slope = im_ref[harm:harm + 1, cols]
            one = which * half + j
            two = one + pair
            rest_ref[pl.ds(one, harm, stride=bodies), :] = jnp.concatenate([re[:, :reals], im[:, :reals]], axis=1)
            rest_ref[pl.ds(two, harm, stride=bodies), :] = jnp.concatenate([re[:, reals:], im[:, reals:]], axis=1)
            slope_ref[pl.ds(one, 1), :] = jnp.concatenate([slope[:, :reals], slope[:, :reals]], axis=1)
            slope_ref[pl.ds(two, 1), :] = jnp.concatenate([slope[:, reals:], slope[:, reals:]], axis=1)

    first = lax.axis_index("body") * bodies
    row = lax.broadcasted_iota(jnp.int32, (bodies, everyone), 0)
    col = lax.broadcasted_iota(jnp.int32, (bodies, everyone), 1)
    mine = col == row + first
    ones = jnp.ones((everyone, group), BF16)
    sign = jnp.where(lax.broadcasted_iota(jnp.int32, (bodies, group), 1) < reals, 1.0, -1.0)
    slope = slope_ref[...]
    for h in range(harm):
        rows = pl.ds(h * bodies, bodies)
        rows_im = pl.ds((harm + h) * bodies, bodies)
        real = jnp.where(mine, imped_ref[0, h], jnp.zeros((), BF16))
        imag = jnp.where(mine, imped_ref[1, h], jnp.zeros((), BF16))
        den = jnp.dot(jnp.concatenate([real, imag], axis=0), ones, preferred_element_type=F32)
        den_re = den[:bodies] + slope
        den_im = den[bodies:]
        inverse = 1.0 / (den_re * den_re + den_im * den_im)
        p_ref[rows, :] = den_re * inverse
        q_ref[rows, :] = den_im * inverse * sign
        vel = jnp.concatenate([velocity_ref[rows, :], velocity_ref[rows_im, :]], axis=1)
        vel_ref[rows, :] = vel
        excite = jnp.concatenate([excite_ref[rows, :], excite_ref[rows_im, :]], axis=1)
        rest_ref[rows, :] = rest_ref[rows, :] - excite + slope * (vel - vel.astype(BF16).astype(F32))


def couple_kernel(harm, bodies, reals, line, imped_ref, *refs):
    pieces, (rest_ref, res_ref, total_ref, held_ref) = refs[:-4], refs[-4:]
    me = lax.axis_index("body")
    sign = jnp.where(lax.broadcasted_iota(jnp.int32, (bodies, 2 * reals), 1) < reals, -1.0, 1.0)
    total = jnp.zeros((8, 2 * reals), F32)
    ends = jnp.logical_or(me == 0, me == 3)
    for h in range(harm):
        rows = pl.ds(h * bodies, bodies)
        if not line:
            vels = pieces[0][:, h].reshape(-1, 2 * reals)
        else:
            slot = h % 4
            held = [ref[rows, :] for ref in pieces]
            for flip, value in ((0, held[0]), (1, held[1]), (3, jnp.where(ends, held[3], held[2])),
                                (2, jnp.where(ends, held[4], held[5]))):
                held_ref[slot, pl.ds(pl.multiple_of((me ^ flip) * bodies, bodies), bodies), :] = value
            vels = held_ref[slot]
        both = imped_ref[:, h].reshape(2 * bodies, imped_ref.shape[3])
        out = jnp.dot(both, vels, preferred_element_type=F32)
        res = out[:bodies] + sign * pltpu.roll(out[bodies:], reals, 1) + rest_ref[rows, :]
        res_ref[rows, :] = res
        total = total + jnp.sum((res * res).reshape(bodies // 8, 8, 2 * reals), axis=0)
    total_ref[...] = jnp.broadcast_to(jnp.sum(total), total_ref.shape)


def finish_kernel(harm, bodies, reals, res_ref, p_ref, q_ref, vel_ref, out_ref):
    rows = out_ref.shape[1]
    at = pl.ds(pl.multiple_of(pl.program_id(0) * rows, rows), rows)
    res = res_ref[at, :]
    new = vel_ref[at, :] - (res * p_ref[at, :] + pltpu.roll(res, reals, 1) * q_ref[at, :])
    out_ref[0] = new[:, :reals]
    out_ref[1] = new[:, reals:]


def rms_kernel(scale, one_ref, two_ref, out_ref):
    mean = (one_ref[...] + two_ref[...]) * scale
    out_ref[0] = jnp.sqrt(mean)[0, 0]


def gather_line(x, again, axis):
    near = lax.ppermute(x, axis, [(0, 1), (1, 0), (2, 3), (3, 2)])
    cross = lax.ppermute(x, axis, [(1, 2), (2, 1)])
    across = lax.ppermute(again, axis, [(0, 3), (3, 0)])
    outer = lax.ppermute(cross, axis, [(1, 0), (2, 3)])
    inner = lax.ppermute(near, axis, [(1, 2), (2, 1)])
    return x, near, cross, across, outer, inner


def params(mib=24):
    return pltpu.CompilerParams(vmem_limit_bytes=mib << 20)


def cost(flops, moved):
    return pl.CostEstimate(flops=flops, bytes_accessed=moved, transcendentals=0)


def make_local(mesh):
    body_count = mesh.shape["body"]

    def local(vel, imped, excite, quad_coef, coul_coef):
        _, harm, bodies, reals = vel.shape
        everyone = imped.shape[3]
        group = 2 * reals
        total_rows = harm * bodies
        forward, inverse = wave_constants(H // harm)
        flat = vel.reshape(2 * total_rows, reals)
        flat_excite = excite.reshape(2 * total_rows, reals)
        dense = jax.ShapeDtypeStruct((total_rows, group), F32)

        def flipped(x, flip):
            return lax.ppermute(x, "harm", [(i, i ^ flip) for i in range(4)])

        low = pl.pallas_call(
            functools.partial(pack_couple, harm, bodies, reals),
            out_shape=jax.ShapeDtypeStruct((total_rows, group), BF16),
            compiler_params=params(),
            cost_estimate=cost(0, 1 << 10),
            name="pack_couple",
        )(flat)
        columns = bodies * reals // 2
        own, send, again = pl.pallas_call(
            functools.partial(pack_time, harm, bodies, reals),
            in_specs=[VMEM],
            out_shape=(
                *[jax.ShapeDtypeStruct((2 * harm, columns), BF16)] * 2,
                jax.ShapeDtypeStruct((total_rows, group), BF16),
            ),
            compiler_params=params(),
            cost_estimate=cost(0, 1 << 10),
            name="pack_time",
        )(flat)
        if body_count == 4:
            pieces = gather_line(low, again, "body")
        else:
            pieces = (lax.all_gather(low, "body").reshape(body_count, harm, bodies, group),)

        far = flipped(own, 2)
        far_core = flipped(send, 3)
        core = flipped(send, 1)

        width = 8 * group
        tile = pl.BlockSpec((2 * harm, width), lambda i: (0, i))
        heights = (2 * harm + 8, harm, harm + 8)
        mine, *other = pl.pallas_call(
            functools.partial(time_kernel, harm, bodies, reals),
            grid=(columns // width,),
            in_specs=[SMEM, SMEM, tile, tile, tile, tile, VMEM, VMEM],
            out_specs=[pl.BlockSpec((height, width), lambda i: (0, i)) for height in heights],
            out_shape=tuple(jax.ShapeDtypeStruct((height, columns), F32) for height in heights),
            scratch_shapes=[pltpu.VMEM((4 * H, width), BF16), pltpu.VMEM((3 * NT, width), BF16)],
            compiler_params=params(),
            cost_estimate=cost(0, 1 << 10),
            name="time_kernel",
        )(quad_coef, coul_coef, own, core, far, far_core, jnp.asarray(forward), jnp.asarray(inverse))
        other = [flipped(part, 1) for part in other]

        rest, factor_p, factor_q, vel_dense = pl.pallas_call(
            functools.partial(prepare_kernel, harm, bodies, reals),
            in_specs=[VMEM] * 6,
            out_shape=(dense,) * 4,
            scratch_shapes=[pltpu.VMEM((bodies, group), F32)],
            compiler_params=params(),
            cost_estimate=cost(0, 1 << 10),
            name="prepare",
        )(imped, mine, *other, flat_excite, flat)

        res, total = pl.pallas_call(
            functools.partial(couple_kernel, harm, bodies, reals, body_count == 4),
            in_specs=[VMEM] * (2 + len(pieces)),
            out_shape=(dense, jax.ShapeDtypeStruct((8, 128), F32)),
            scratch_shapes=[pltpu.VMEM((4, everyone, group), BF16)],
            compiler_params=params(),
            cost_estimate=cost(0, 1 << 10),
            name="couple",
        )(imped, *pieces, rest)

        steps = 2
        rows = total_rows // steps
        new = pl.pallas_call(
            functools.partial(finish_kernel, harm, bodies, reals),
            grid=(steps,),
            in_specs=[VMEM] * 4,
            out_specs=pl.BlockSpec((2, rows, reals), lambda i: (0, i, 0)),
            out_shape=jax.ShapeDtypeStruct((2, total_rows, reals), F32),
            compiler_params=params(),
            cost_estimate=cost(0, 1 << 10),
            name="finish",
        )(res, factor_p, factor_q, vel_dense)

        total = total + flipped(total, 1)
        got = flipped(total, 3)
        flip = 1
        while flip < body_count:
            total = total + got
            pairs = [(4 * i + j, 4 * (i ^ flip) + (j ^ 1)) for i in range(body_count) for j in range(4)]
            got = lax.ppermute(total, ("body", "harm"), pairs)
            flip *= 2
        rms = pl.pallas_call(
            functools.partial(rms_kernel, 1.0 / (2.0 * H * everyone * reals)),
            in_specs=[VMEM] * 2,
            out_specs=SMEM,
            out_shape=jax.ShapeDtypeStruct((1,), F32),
            compiler_params=params(),
            name="rms",
        )(total, got)
        return new.reshape(vel.shape), rms

    return local


def solution(mesh):
    in_specs = (
        P(None, "harm", "body", "sea"),
        P(None, "harm", "body", None),
        P(None, "harm", "body", "sea"),
        P("body"),
        P("body"),
    )
    out_specs = (P(None, "harm", "body", "sea"), P("sea"))
    return jax.shard_map(make_local(mesh), mesh=mesh, in_specs=in_specs, out_specs=out_specs, check_vma=False)
```

```python
import functools
import math

import ml_dtypes
import numpy as np
import jax
import jax.numpy as jnp
from jax import lax
from jax.experimental import pallas as pl
from jax.experimental.pallas import tpu as pltpu
from jax.sharding import PartitionSpec as P

H = 128
NT = 512
DELTA = 0.1
F32 = jnp.float32
BF16 = jnp.bfloat16
VMEM = pl.BlockSpec(memory_space=pltpu.VMEM)
SMEM = pl.BlockSpec(memory_space=pltpu.SMEM)


def split(x):
    high = x.astype(BF16)
    return high, (x - high.astype(F32)).astype(BF16)


def wave_constants(groups):
    k = np.arange(1, H + 1)
    phase = np.arange(NT)[None, :] * k[:, None] % NT
    angle = phase * (2.0 * math.pi / NT)
    waves = np.stack([np.cos(angle), -np.sin(angle)]).reshape(2, groups, H // groups, NT)
    table = (np.swapaxes(waves, 0, 1).reshape(2 * H, NT) / math.sqrt(H)).astype(np.float32)
    high = table.astype(ml_dtypes.bfloat16)
    low = (table - high.astype(np.float32)).astype(ml_dtypes.bfloat16)
    return np.concatenate([high.T, low.T], axis=1), np.concatenate([high, low, high], axis=1)


def pack_couple(harm, bodies, reals, vel_ref, out_ref):
    for h in range(harm):
        rows = pl.ds(h * bodies, bodies)
        re = vel_ref[rows, :]
        im = vel_ref[pl.ds((harm + h) * bodies, bodies), :]
        out_ref[rows, :] = jnp.concatenate([re, im], axis=1).astype(BF16)


def pack_time(harm, bodies, reals, vel_ref, own_ref, send_ref, again_ref):
    core = lax.axis_index("harm") % 2
    half = bodies // 2
    pair = bodies // 4
    for which, out_ref in ((core, own_ref), (1 - core, send_ref)):
        for j in range(pair):
            one = vel_ref[pl.ds(which * half + j, 2 * harm, stride=bodies), :]
            two = vel_ref[pl.ds(which * half + pair + j, 2 * harm, stride=bodies), :]
            out_ref[:, pl.ds(j * 2 * reals, 2 * reals)] = jnp.concatenate([one, two], axis=1).astype(BF16)
    pack_couple(harm, bodies, reals, vel_ref, again_ref)


def time_kernel(harm, bodies, reals, quad_ref, coul_ref, own_ref, core_ref, far_ref, far_core_ref, fwd_ref, inv_ref,
                mine_ref, other_ref, other_im_ref, held_ref, force_ref):
    step = pl.program_id(0)
    me = lax.axis_index("harm")
    core = me % 2
    size = 2 * harm
    width = own_ref.shape[1]
    group = 2 * reals
    pair = bodies // 4
    base = core * (bodies // 2) + step * (width // group)
    small = DELTA * DELTA

    for flip, ref in enumerate((own_ref, core_ref, far_ref, far_core_ref)):
        value = ref[...]
        first = pl.multiple_of((me ^ flip) * size, size)
        held_ref[pl.ds(first, size), :] = value
        held_ref[pl.ds(first + 2 * H, size), :] = value

    lane = lax.broadcasted_iota(jnp.int32, (1, group), 1)
    quads, couls = [], []
    for g in range(width // group):
        quads.append(jnp.where(lane < reals, quad_ref[base + g], quad_ref[base + g + pair]))
        couls.append(jnp.where(lane < reals, coul_ref[base + g], coul_ref[base + g + pair]))
    quad = jnp.concatenate(quads, axis=1)
    coul = jnp.concatenate(couls, axis=1)

    signal = jnp.dot(fwd_ref[...], held_ref[...], preferred_element_type=F32)
    square = signal * signal + small
    inverse = lax.rsqrt(square)
    root = square * inverse
    high, low = split(signal * (quad * root + coul * inverse))
    force_ref[:NT] = high
    force_ref[NT:2 * NT] = high
    force_ref[2 * NT:] = low
    roots = jnp.sum(root, axis=0, keepdims=True)
    inverses = jnp.sum(inverse, axis=0, keepdims=True)
    cubes = jnp.sum(inverse * inverse * inverse, axis=0, keepdims=True)
    mean = (quad * (2.0 * roots - small * inverses) + coul * (small * cubes)) * (1.0 / NT)

    first = pl.multiple_of((me // 2) * 2 * size, 2 * size)
    back = jnp.dot(inv_ref[pl.ds(first, 2 * size), :], force_ref[...], preferred_element_type=F32) * (2.0 * H / NT)
    lower = core == 0
    mine_ref[:size] = jnp.where(lower, back[:size], back[size:])
    other = jnp.where(lower, back[size:], back[:size])
    slope = jnp.broadcast_to(mean, (8, width))
    mine_ref[size:] = slope
    other_ref[...] = other[:harm]
    other_im_ref[:harm] = other[harm:]
    other_im_ref[harm:] = slope


def prepare_kernel(harm, bodies, reals, imped_ref, mine_ref, other_re_ref, other_im_ref, excite_ref, velocity_ref,
                   rest_ref, p_ref, q_ref, vel_ref, slope_ref):
    everyone = imped_ref.shape[3]
    group = 2 * reals
    half = bodies // 2
    pair = bodies // 4
    core = lax.axis_index("harm") % 2
    mine_re_ref, mine_im_ref = mine_ref.at[:harm], mine_ref.at[harm:]
    for which, re_ref, im_ref in ((core, mine_re_ref, mine_im_ref), (1 - core, other_re_ref, other_im_ref)):
        for j in range(pair):
            cols = slice(j * group, (j + 1) * group)
            re = re_ref[:, cols]
            im = im_ref[:harm, cols]
            slope = im_ref[harm:harm + 1, cols]
            one = which * half + j
            two = one + pair
            rest_ref[pl.ds(one, harm, stride=bodies), :] = jnp.concatenate([re[:, :reals], im[:, :reals]], axis=1)
            rest_ref[pl.ds(two, harm, stride=bodies), :] = jnp.concatenate([re[:, reals:], im[:, reals:]], axis=1)
            slope_ref[pl.ds(one, 1), :] = jnp.concatenate([slope[:, :reals], slope[:, :reals]], axis=1)
            slope_ref[pl.ds(two, 1), :] = jnp.concatenate([slope[:, reals:], slope[:, reals:]], axis=1)

    first = lax.axis_index("body") * bodies
    row = lax.broadcasted_iota(jnp.int32, (bodies, everyone), 0)
    col = lax.broadcasted_iota(jnp.int32, (bodies, everyone), 1)
    mine = col == row + first
    ones = jnp.ones((everyone, group), BF16)
    sign = jnp.where(lax.broadcasted_iota(jnp.int32, (bodies, group), 1) < reals, 1.0, -1.0)
    slope = slope_ref[...]
    for h in range(harm):
        rows = pl.ds(h * bodies, bodies)
        rows_im = pl.ds((harm + h) * bodies, bodies)
        real = jnp.where(mine, imped_ref[0, h], jnp.zeros((), BF16))
        imag = jnp.where(mine, imped_ref[1, h], jnp.zeros((), BF16))
        den = jnp.dot(jnp.concatenate([real, imag], axis=0), ones, preferred_element_type=F32)
        den_re = den[:bodies] + slope
        den_im = den[bodies:]
        inverse = 1.0 / (den_re * den_re + den_im * den_im)
        p_ref[rows, :] = den_re * inverse
        q_ref[rows, :] = den_im * inverse * sign
        vel = jnp.concatenate([velocity_ref[rows, :], velocity_ref[rows_im, :]], axis=1)
        vel_ref[rows, :] = vel
        excite = jnp.concatenate([excite_ref[rows, :], excite_ref[rows_im, :]], axis=1)
        rest_ref[rows, :] = rest_ref[rows, :] - excite + slope * (vel - vel.astype(BF16).astype(F32))


def couple_kernel(harm, bodies, reals, line, imped_ref, *refs):
    pieces, (rest_ref, res_ref, total_ref, held_ref) = refs[:-4], refs[-4:]
    me = lax.axis_index("body")
    sign = jnp.where(lax.broadcasted_iota(jnp.int32, (bodies, 2 * reals), 1) < reals, -1.0, 1.0)
    total = jnp.zeros((8, 2 * reals), F32)
    ends = jnp.logical_or(me == 0, me == 3)
    for h in range(harm):
        rows = pl.ds(h * bodies, bodies)
        if not line:
            vels = pieces[0][:, h].reshape(-1, 2 * reals)
        else:
            slot = h % 4
            held = [ref[rows, :] for ref in pieces]
            for flip, value in ((0, held[0]), (1, held[1]), (3, jnp.where(ends, held[3], held[2])),
                                (2, jnp.where(ends, held[4], held[5]))):
                held_ref[slot, pl.ds(pl.multiple_of((me ^ flip) * bodies, bodies), bodies), :] = value
            vels = held_ref[slot]
        both = imped_ref[:, h].reshape(2 * bodies, imped_ref.shape[3])
        out = jnp.dot(both, vels, preferred_element_type=F32)
        res = out[:bodies] + sign * pltpu.roll(out[bodies:], reals, 1) + rest_ref[rows, :]
        res_ref[rows, :] = res
        total = total + jnp.sum((res * res).reshape(bodies // 8, 8, 2 * reals), axis=0)
    total_ref[...] = jnp.broadcast_to(jnp.sum(total), total_ref.shape)


def finish_kernel(harm, bodies, reals, res_ref, p_ref, q_ref, vel_ref, out_ref):
    rows = out_ref.shape[1]
    at = pl.ds(pl.multiple_of(pl.program_id(0) * rows, rows), rows)
    res = res_ref[at, :]
    new = vel_ref[at, :] - (res * p_ref[at, :] + pltpu.roll(res, reals, 1) * q_ref[at, :])
    out_ref[0] = new[:, :reals]
    out_ref[1] = new[:, reals:]


def rms_kernel(scale, *refs):
    *parts, out_ref = refs
    mean = sum(part[...] for part in parts) * scale
    out_ref[0] = jnp.sqrt(mean)[0, 0]


def gather_line(x, again, axis):
    near = lax.ppermute(x, axis, [(0, 1), (1, 0), (2, 3), (3, 2)])
    cross = lax.ppermute(x, axis, [(1, 2), (2, 1)])
    across = lax.ppermute(again, axis, [(0, 3), (3, 0)])
    outer = lax.ppermute(cross, axis, [(1, 0), (2, 3)])
    inner = lax.ppermute(near, axis, [(1, 2), (2, 1)])
    return x, near, cross, across, outer, inner


def params(mib=24):
    return pltpu.CompilerParams(vmem_limit_bytes=mib << 20)


def cost(flops, moved):
    return pl.CostEstimate(flops=flops, bytes_accessed=moved, transcendentals=0)


def make_local(mesh):
    body_count = mesh.shape["body"]

    def local(vel, imped, excite, quad_coef, coul_coef):
        _, harm, bodies, reals = vel.shape
        everyone = imped.shape[3]
        group = 2 * reals
        total_rows = harm * bodies
        forward, inverse = wave_constants(H // harm)
        flat = vel.reshape(2 * total_rows, reals)
        flat_excite = excite.reshape(2 * total_rows, reals)
        dense = jax.ShapeDtypeStruct((total_rows, group), F32)

        def flipped(x, flip):
            return lax.ppermute(x, "harm", [(i, i ^ flip) for i in range(4)])

        low = pl.pallas_call(
            functools.partial(pack_couple, harm, bodies, reals),
            out_shape=jax.ShapeDtypeStruct((total_rows, group), BF16),
            compiler_params=params(),
            cost_estimate=cost(0, 1 << 10),
            name="pack_couple",
        )(flat)
        columns = bodies * reals // 2
        own, send, again = pl.pallas_call(
            functools.partial(pack_time, harm, bodies, reals),
            in_specs=[VMEM],
            out_shape=(
                *[jax.ShapeDtypeStruct((2 * harm, columns), BF16)] * 2,
                jax.ShapeDtypeStruct((total_rows, group), BF16),
            ),
            compiler_params=params(),
            cost_estimate=cost(0, 1 << 10),
            name="pack_time",
        )(flat)
        if body_count == 4:
            pieces = gather_line(low, again, "body")
        else:
            pieces = (lax.all_gather(low, "body").reshape(body_count, harm, bodies, group),)

        far = flipped(own, 2)
        far_core = flipped(send, 3)
        core = flipped(send, 1)

        width = 8 * group
        tile = pl.BlockSpec((2 * harm, width), lambda i: (0, i))
        heights = (2 * harm + 8, harm, harm + 8)
        mine, *other = pl.pallas_call(
            functools.partial(time_kernel, harm, bodies, reals),
            grid=(columns // width,),
            in_specs=[SMEM, SMEM, tile, tile, tile, tile, VMEM, VMEM],
            out_specs=[pl.BlockSpec((height, width), lambda i: (0, i)) for height in heights],
            out_shape=tuple(jax.ShapeDtypeStruct((height, columns), F32) for height in heights),
            scratch_shapes=[pltpu.VMEM((4 * H, width), BF16), pltpu.VMEM((3 * NT, width), BF16)],
            compiler_params=params(),
            cost_estimate=cost(0, 1 << 10),
            name="time_kernel",
        )(quad_coef, coul_coef, own, core, far, far_core, jnp.asarray(forward), jnp.asarray(inverse))
        other = [flipped(part, 1) for part in other]

        rest, factor_p, factor_q, vel_dense = pl.pallas_call(
            functools.partial(prepare_kernel, harm, bodies, reals),
            in_specs=[VMEM] * 6,
            out_shape=(dense,) * 4,
            scratch_shapes=[pltpu.VMEM((bodies, group), F32)],
            compiler_params=params(),
            cost_estimate=cost(0, 1 << 10),
            name="prepare",
        )(imped, mine, *other, flat_excite, flat)

        res, total = pl.pallas_call(
            functools.partial(couple_kernel, harm, bodies, reals, body_count == 4),
            in_specs=[VMEM] * (2 + len(pieces)),
            out_shape=(dense, jax.ShapeDtypeStruct((8, 128), F32)),
            scratch_shapes=[pltpu.VMEM((4, everyone, group), BF16)],
            compiler_params=params(),
            cost_estimate=cost(0, 1 << 10),
            name="couple",
        )(imped, *pieces, rest)

        steps = 2
        rows = total_rows // steps
        new = pl.pallas_call(
            functools.partial(finish_kernel, harm, bodies, reals),
            grid=(steps,),
            in_specs=[VMEM] * 4,
            out_specs=pl.BlockSpec((2, rows, reals), lambda i: (0, i, 0)),
            out_shape=jax.ShapeDtypeStruct((2, total_rows, reals), F32),
            compiler_params=params(),
            cost_estimate=cost(0, 1 << 10),
            name="finish",
        )(res, factor_p, factor_q, vel_dense)

        total = total + flipped(total, 1)
        total = total + flipped(total, 3)

        def crossed(flip):
            pairs = [(4 * i + j, 4 * (i ^ flip) + (j ^ 1)) for i in range(body_count) for j in range(4)]
            return lax.ppermute(total, ("body", "harm"), pairs)

        for bit in range(2, body_count.bit_length() - 1):
            total = total + crossed(1 << bit)
        got = [crossed(flip) for flip in (3, 2, 1)]
        rms = pl.pallas_call(
            functools.partial(rms_kernel, 1.0 / (2.0 * H * everyone * reals)),
            in_specs=[VMEM] * (1 + len(got)),
            out_specs=SMEM,
            out_shape=jax.ShapeDtypeStruct((1,), F32),
            compiler_params=params(),
            name="rms",
        )(total, *got)
        return new.reshape(vel.shape), rms

    return local


def solution(mesh):
    in_specs = (
        P(None, "harm", "body", "sea"),
        P(None, "harm", "body", None),
        P(None, "harm", "body", "sea"),
        P("body"),
        P("body"),
    )
    out_specs = (P(None, "harm", "body", "sea"), P("sea"))
    return jax.shard_map(make_local(mesh), mesh=mesh, in_specs=in_specs, out_specs=out_specs, check_vma=False)
```

```python
import functools
import math

import ml_dtypes
import numpy as np
import jax
import jax.numpy as jnp
from jax import lax
from jax.experimental import pallas as pl
from jax.experimental.pallas import tpu as pltpu
from jax.sharding import PartitionSpec as P

H = 128
NT = 512
DELTA = 0.1
F32 = jnp.float32
BF16 = jnp.bfloat16
VMEM = pl.BlockSpec(memory_space=pltpu.VMEM)
SMEM = pl.BlockSpec(memory_space=pltpu.SMEM)


def split(x):
    high = x.astype(BF16)
    return high, (x - high.astype(F32)).astype(BF16)


def wave_constants(groups):
    k = np.arange(1, H + 1)
    phase = np.arange(NT)[None, :] * k[:, None] % NT
    angle = phase * (2.0 * math.pi / NT)
    waves = np.stack([np.cos(angle), -np.sin(angle)]).reshape(2, groups, H // groups, NT)
    table = (np.swapaxes(waves, 0, 1).reshape(2 * H, NT) / math.sqrt(H)).astype(np.float32)
    high = table.astype(ml_dtypes.bfloat16)
    low = (table - high.astype(np.float32)).astype(ml_dtypes.bfloat16)
    return np.concatenate([high.T, low.T], axis=1), np.concatenate([high, low, high], axis=1)


def pack_couple(harm, bodies, reals, vel_ref, out_ref):
    for h in range(harm):
        rows = pl.ds(h * bodies, bodies)
        re = vel_ref[rows, :]
        im = vel_ref[pl.ds((harm + h) * bodies, bodies), :]
        out_ref[rows, :] = jnp.concatenate([re, im], axis=1).astype(BF16)


def pack_time(harm, bodies, reals, vel_ref, own_ref, send_ref, again_ref):
    core = lax.axis_index("harm") % 2
    half = bodies // 2
    pair = bodies // 4
    for which, out_ref in ((core, own_ref), (1 - core, send_ref)):
        for j in range(pair):
            one = vel_ref[pl.ds(which * half + j, 2 * harm, stride=bodies), :]
            two = vel_ref[pl.ds(which * half + pair + j, 2 * harm, stride=bodies), :]
            out_ref[:, pl.ds(j * 2 * reals, 2 * reals)] = jnp.concatenate([one, two], axis=1).astype(BF16)
    pack_couple(harm, bodies, reals, vel_ref, again_ref)


def time_kernel(harm, bodies, reals, quad_ref, coul_ref, own_ref, core_ref, far_ref, far_core_ref, fwd_ref, inv_ref,
                mine_ref, other_ref, other_im_ref, held_ref, force_ref):
    step = pl.program_id(0)
    me = lax.axis_index("harm")
    core = me % 2
    size = 2 * harm
    width = own_ref.shape[1]
    group = 2 * reals
    pair = bodies // 4
    base = core * (bodies // 2) + step * (width // group)
    small = DELTA * DELTA

    for flip, ref in enumerate((own_ref, core_ref, far_ref, far_core_ref)):
        value = ref[...]
        first = pl.multiple_of((me ^ flip) * size, size)
        held_ref[pl.ds(first, size), :] = value
        held_ref[pl.ds(first + 2 * H, size), :] = value

    lane = lax.broadcasted_iota(jnp.int32, (1, group), 1)
    quads, couls = [], []
    for g in range(width // group):
        quads.append(jnp.where(lane < reals, quad_ref[base + g], quad_ref[base + g + pair]))
        couls.append(jnp.where(lane < reals, coul_ref[base + g], coul_ref[base + g + pair]))
    quad = jnp.concatenate(quads, axis=1)
    coul = jnp.concatenate(couls, axis=1)

    signal = jnp.dot(fwd_ref[...], held_ref[...], preferred_element_type=F32)
    square = signal * signal + small
    inverse = lax.rsqrt(square)
    root = square * inverse
    high, low = split(signal * (quad * root + coul * inverse))
    force_ref[:NT] = high
    force_ref[NT:2 * NT] = high
    force_ref[2 * NT:] = low
    roots = jnp.sum(root, axis=0, keepdims=True)
    inverses = jnp.sum(inverse, axis=0, keepdims=True)
    cubes = jnp.sum(inverse * inverse * inverse, axis=0, keepdims=True)
    mean = (quad * (2.0 * roots - small * inverses) + coul * (small * cubes)) * (1.0 / NT)

    first = pl.multiple_of((me // 2) * 2 * size, 2 * size)
    back = jnp.dot(inv_ref[pl.ds(first, 2 * size), :], force_ref[...], preferred_element_type=F32) * (2.0 * H / NT)
    lower = core == 0
    mine_ref[:size] = jnp.where(lower, back[:size], back[size:])
    other = jnp.where(lower, back[size:], back[:size])
    slope = jnp.broadcast_to(mean, (8, width))
    mine_ref[size:] = slope
    other_ref[...] = other[:harm]
    other_im_ref[:harm] = other[harm:]
    other_im_ref[harm:] = slope


def prepare_kernel(harm, bodies, reals, imped_ref, mine_ref, other_re_ref, other_im_ref, excite_ref, velocity_ref,
                   rest_ref, p_ref, q_ref, vel_ref, slope_ref):
    everyone = imped_ref.shape[3]
    group = 2 * reals
    half = bodies // 2
    pair = bodies // 4
    core = lax.axis_index("harm") % 2
    mine_re_ref, mine_im_ref = mine_ref.at[:harm], mine_ref.at[harm:]
    for which, re_ref, im_ref in ((core, mine_re_ref, mine_im_ref), (1 - core, other_re_ref, other_im_ref)):
        for j in range(pair):
            cols = slice(j * group, (j + 1) * group)
            re = re_ref[:, cols]
            im = im_ref[:harm, cols]
            slope = im_ref[harm:harm + 1, cols]
            one = which * half + j
            two = one + pair
            rest_ref[pl.ds(one, harm, stride=bodies), :] = jnp.concatenate([re[:, :reals], im[:, :reals]], axis=1)
            rest_ref[pl.ds(two, harm, stride=bodies), :] = jnp.concatenate([re[:, reals:], im[:, reals:]], axis=1)
            slope_ref[pl.ds(one, 1), :] = jnp.concatenate([slope[:, :reals], slope[:, :reals]], axis=1)
            slope_ref[pl.ds(two, 1), :] = jnp.concatenate([slope[:, reals:], slope[:, reals:]], axis=1)

    first = lax.axis_index("body") * bodies
    row = lax.broadcasted_iota(jnp.int32, (bodies, everyone), 0)
    col = lax.broadcasted_iota(jnp.int32, (bodies, everyone), 1)
    mine = col == row + first
    ones = jnp.ones((everyone, group), BF16)
    sign = jnp.where(lax.broadcasted_iota(jnp.int32, (bodies, group), 1) < reals, 1.0, -1.0)
    slope = slope_ref[...]
    for h in range(harm):
        rows = pl.ds(h * bodies, bodies)
        rows_im = pl.ds((harm + h) * bodies, bodies)
        real = jnp.where(mine, imped_ref[0, h], jnp.zeros((), BF16))
        imag = jnp.where(mine, imped_ref[1, h], jnp.zeros((), BF16))
        den = jnp.dot(jnp.concatenate([real, imag], axis=0), ones, preferred_element_type=F32)
        den_re = den[:bodies] + slope
        den_im = den[bodies:]
        inverse = 1.0 / (den_re * den_re + den_im * den_im)
        p_ref[rows, :] = den_re * inverse
        q_ref[rows, :] = den_im * inverse * sign
        vel = jnp.concatenate([velocity_ref[rows, :], velocity_ref[rows_im, :]], axis=1)
        vel_ref[rows, :] = vel
        excite = jnp.concatenate([excite_ref[rows, :], excite_ref[rows_im, :]], axis=1)
        rest_ref[rows, :] = rest_ref[rows, :] - excite + slope * (vel - vel.astype(BF16).astype(F32))


def coupling(imped, vels, bodies, reals):
    sign = jnp.where(lax.broadcasted_iota(jnp.int32, (bodies, 2 * reals), 1) < reals, -1.0, 1.0)
    out = jnp.dot(imped.reshape(2 * bodies, imped.shape[2]), vels, preferred_element_type=F32)
    return out[:bodies] + sign * pltpu.roll(out[bodies:], reals, 1)


def at_ends(me):
    return jnp.logical_or(me == 0, me == 3)


def partial_kernel(harm, bodies, reals, imped_ref, own_ref, near_ref, cross_ref, across_ref, rest_ref, out_ref, held_ref):
    me = lax.axis_index("body")
    ends = at_ends(me)
    held_ref[...] = jnp.zeros_like(held_ref)
    for h in range(harm):
        rows = pl.ds(h * bodies, bodies)
        slot = h % 4
        for flip, value in ((0, own_ref[rows, :]), (1, near_ref[rows, :]),
                            (3, jnp.where(ends, across_ref[rows, :], cross_ref[rows, :]))):
            held_ref[slot, pl.ds(pl.multiple_of((me ^ flip) * bodies, bodies), bodies), :] = value
        out_ref[rows, :] = rest_ref[rows, :] + coupling(imped_ref[:, h], held_ref[slot], bodies, reals)


def couple_kernel(harm, bodies, reals, line, imped_ref, *refs):
    pieces, (rest_ref, res_ref, total_ref) = refs[:-3], refs[-3:]
    total = jnp.zeros((8, 2 * reals), F32)
    if line:
        me = lax.axis_index("body")
        ends = at_ends(me)
        source = me ^ 2
        lower = source % 2 == 0
        none = jnp.zeros((bodies, 2 * reals), BF16)
        cols = pl.ds(pl.multiple_of((source // 2) * 2 * bodies, 2 * bodies), 2 * bodies)
    for h in range(harm):
        rows = pl.ds(h * bodies, bodies)
        if line:
            value = jnp.where(ends, pieces[0][rows, :], pieces[1][rows, :])
            vels = jnp.concatenate([jnp.where(lower, value, none), jnp.where(lower, none, value)], axis=0)
            imped = imped_ref[:, h, :, cols]
        else:
            vels = pieces[0][:, h].reshape(-1, 2 * reals)
            imped = imped_ref[:, h]
        res = coupling(imped, vels, bodies, reals) + rest_ref[rows, :]
        res_ref[rows, :] = res
        total = total + jnp.sum((res * res).reshape(bodies // 8, 8, 2 * reals), axis=0)
    total_ref[...] = jnp.broadcast_to(jnp.sum(total), total_ref.shape)


def finish_kernel(harm, bodies, reals, res_ref, p_ref, q_ref, vel_ref, out_ref):
    rows = out_ref.shape[1]
    at = pl.ds(pl.multiple_of(pl.program_id(0) * rows, rows), rows)
    res = res_ref[at, :]
    new = vel_ref[at, :] - (res * p_ref[at, :] + pltpu.roll(res, reals, 1) * q_ref[at, :])
    out_ref[0] = new[:, :reals]
    out_ref[1] = new[:, reals:]


def rms_kernel(scale, *refs):
    *parts, out_ref = refs
    mean = sum(part[...] for part in parts) * scale
    out_ref[0] = jnp.sqrt(mean)[0, 0]


def gather_line(x, again, axis):
    near = lax.ppermute(x, axis, [(0, 1), (1, 0), (2, 3), (3, 2)])
    cross = lax.ppermute(x, axis, [(1, 2), (2, 1)])
    across = lax.ppermute(again, axis, [(0, 3), (3, 0)])
    outer = lax.ppermute(cross, axis, [(1, 0), (2, 3)])
    inner = lax.ppermute(near, axis, [(1, 2), (2, 1)])
    return x, near, cross, across, outer, inner


def params(mib=24):
    return pltpu.CompilerParams(vmem_limit_bytes=mib << 20)


def cost(flops, moved):
    return pl.CostEstimate(flops=flops, bytes_accessed=moved, transcendentals=0)


def make_local(mesh):
    body_count = mesh.shape["body"]

    def local(vel, imped, excite, quad_coef, coul_coef):
        _, harm, bodies, reals = vel.shape
        everyone = imped.shape[3]
        group = 2 * reals
        total_rows = harm * bodies
        forward, inverse = wave_constants(H // harm)
        flat = vel.reshape(2 * total_rows, reals)
        flat_excite = excite.reshape(2 * total_rows, reals)
        dense = jax.ShapeDtypeStruct((total_rows, group), F32)

        def flipped(x, flip):
            return lax.ppermute(x, "harm", [(i, i ^ flip) for i in range(4)])

        low = pl.pallas_call(
            functools.partial(pack_couple, harm, bodies, reals),
            out_shape=jax.ShapeDtypeStruct((total_rows, group), BF16),
            compiler_params=params(),
            cost_estimate=cost(0, 1 << 10),
            name="pack_couple",
        )(flat)
        columns = bodies * reals // 2
        own, send, again = pl.pallas_call(
            functools.partial(pack_time, harm, bodies, reals),
            in_specs=[VMEM],
            out_shape=(
                *[jax.ShapeDtypeStruct((2 * harm, columns), BF16)] * 2,
                jax.ShapeDtypeStruct((total_rows, group), BF16),
            ),
            compiler_params=params(),
            cost_estimate=cost(0, 1 << 10),
            name="pack_time",
        )(flat)
        if body_count == 4:
            pieces = gather_line(low, again, "body")
        else:
            pieces = (lax.all_gather(low, "body").reshape(body_count, harm, bodies, group),)

        far = flipped(own, 2)
        far_core = flipped(send, 3)
        core = flipped(send, 1)

        width = 8 * group
        tile = pl.BlockSpec((2 * harm, width), lambda i: (0, i))
        heights = (2 * harm + 8, harm, harm + 8)
        mine, *other = pl.pallas_call(
            functools.partial(time_kernel, harm, bodies, reals),
            grid=(columns // width,),
            in_specs=[SMEM, SMEM, tile, tile, tile, tile, VMEM, VMEM],
            out_specs=[pl.BlockSpec((height, width), lambda i: (0, i)) for height in heights],
            out_shape=tuple(jax.ShapeDtypeStruct((height, columns), F32) for height in heights),
            scratch_shapes=[pltpu.VMEM((4 * H, width), BF16), pltpu.VMEM((3 * NT, width), BF16)],
            compiler_params=params(),
            cost_estimate=cost(0, 1 << 10),
            name="time_kernel",
        )(quad_coef, coul_coef, own, core, far, far_core, jnp.asarray(forward), jnp.asarray(inverse))
        other = [flipped(part, 1) for part in other]

        rest, factor_p, factor_q, vel_dense = pl.pallas_call(
            functools.partial(prepare_kernel, harm, bodies, reals),
            in_specs=[VMEM] * 6,
            out_shape=(dense,) * 4,
            scratch_shapes=[pltpu.VMEM((bodies, group), F32)],
            compiler_params=params(),
            cost_estimate=cost(0, 1 << 10),
            name="prepare",
        )(imped, mine, *other, flat_excite, flat)

        if body_count == 4:
            rest = pl.pallas_call(
                functools.partial(partial_kernel, harm, bodies, reals),
                in_specs=[VMEM] * 6,
                out_shape=dense,
                scratch_shapes=[pltpu.VMEM((4, everyone, group), BF16)],
                compiler_params=params(),
                cost_estimate=cost(0, 1 << 10),
                name="partial",
            )(imped, *pieces[:4], rest)
            pieces = pieces[4:]
        res, total = pl.pallas_call(
            functools.partial(couple_kernel, harm, bodies, reals, body_count == 4),
            in_specs=[VMEM] * (2 + len(pieces)),
            out_shape=(dense, jax.ShapeDtypeStruct((8, 128), F32)),
            compiler_params=params(),
            cost_estimate=cost(0, 1 << 10),
            name="couple",
        )(imped, *pieces, rest)

        steps = 2
        rows = total_rows // steps
        new = pl.pallas_call(
            functools.partial(finish_kernel, harm, bodies, reals),
            grid=(steps,),
            in_specs=[VMEM] * 4,
            out_specs=pl.BlockSpec((2, rows, reals), lambda i: (0, i, 0)),
            out_shape=jax.ShapeDtypeStruct((2, total_rows, reals), F32),
            compiler_params=params(),
            cost_estimate=cost(0, 1 << 10),
            name="finish",
        )(res, factor_p, factor_q, vel_dense)

        total = total + flipped(total, 1)
        total = total + flipped(total, 3)

        def crossed(flip):
            pairs = [(4 * i + j, 4 * (i ^ flip) + (j ^ 1)) for i in range(body_count) for j in range(4)]
            return lax.ppermute(total, ("body", "harm"), pairs)

        for bit in range(2, body_count.bit_length() - 1):
            total = total + crossed(1 << bit)
        got = [crossed(flip) for flip in (3, 2, 1)]
        rms = pl.pallas_call(
            functools.partial(rms_kernel, 1.0 / (2.0 * H * everyone * reals)),
            in_specs=[VMEM] * (1 + len(got)),
            out_specs=SMEM,
            out_shape=jax.ShapeDtypeStruct((1,), F32),
            compiler_params=params(),
            name="rms",
        )(total, *got)
        return new.reshape(vel.shape), rms

    return local


def solution(mesh):
    in_specs = (
        P(None, "harm", "body", "sea"),
        P(None, "harm", "body", None),
        P(None, "harm", "body", "sea"),
        P("body"),
        P("body"),
    )
    out_specs = (P(None, "harm", "body", "sea"), P("sea"))
    return jax.shard_map(make_local(mesh), mesh=mesh, in_specs=in_specs, out_specs=out_specs, check_vma=False)
```

```python
import functools
import math

import ml_dtypes
import numpy as np
import jax
import jax.numpy as jnp
from jax import lax
from jax.experimental import pallas as pl
from jax.experimental.pallas import tpu as pltpu
from jax.sharding import PartitionSpec as P

H = 128
NT = 512
DELTA = 0.1
F32 = jnp.float32
BF16 = jnp.bfloat16
VMEM = pl.BlockSpec(memory_space=pltpu.VMEM)
SMEM = pl.BlockSpec(memory_space=pltpu.SMEM)


def split(x):
    high = x.astype(BF16)
    return high, (x - high.astype(F32)).astype(BF16)


def wave_constants(groups):
    k = np.arange(1, H + 1)
    phase = np.arange(NT)[None, :] * k[:, None] % NT
    angle = phase * (2.0 * math.pi / NT)
    waves = np.stack([np.cos(angle), -np.sin(angle)]).reshape(2, groups, H // groups, NT)
    table = (np.swapaxes(waves, 0, 1).reshape(2 * H, NT) / math.sqrt(H)).astype(np.float32)
    high = table.astype(ml_dtypes.bfloat16)
    low = (table - high.astype(np.float32)).astype(ml_dtypes.bfloat16)
    return np.concatenate([high.T, low.T], axis=1), np.concatenate([high, low, high], axis=1)


def pack_couple(harm, bodies, reals, vel_ref, out_ref):
    for h in range(harm):
        rows = pl.ds(h * bodies, bodies)
        re = vel_ref[rows, :]
        im = vel_ref[pl.ds((harm + h) * bodies, bodies), :]
        out_ref[rows, :] = jnp.concatenate([re, im], axis=1).astype(BF16)


def pack_time(harm, bodies, reals, vel_ref, own_ref, send_ref):
    core = lax.axis_index("harm") % 2
    half = bodies // 2
    pair = bodies // 4
    for which, out_ref in ((core, own_ref), (1 - core, send_ref)):
        for j in range(pair):
            one = vel_ref[pl.ds(which * half + j, 2 * harm, stride=bodies), :]
            two = vel_ref[pl.ds(which * half + pair + j, 2 * harm, stride=bodies), :]
            out_ref[:, pl.ds(j * 2 * reals, 2 * reals)] = jnp.concatenate([one, two], axis=1).astype(BF16)


def time_kernel(harm, bodies, reals, quad_ref, coul_ref, own_ref, core_ref, far_ref, far_core_ref, fwd_ref, inv_ref,
                mine_ref, other_ref, other_im_ref, held_ref, force_ref):
    step = pl.program_id(0)
    me = lax.axis_index("harm")
    core = me % 2
    size = 2 * harm
    width = own_ref.shape[1]
    group = 2 * reals
    pair = bodies // 4
    base = core * (bodies // 2) + step * (width // group)
    small = DELTA * DELTA

    for flip, ref in enumerate((own_ref, core_ref, far_ref, far_core_ref)):
        value = ref[...]
        first = pl.multiple_of((me ^ flip) * size, size)
        held_ref[pl.ds(first, size), :] = value
        held_ref[pl.ds(first + 2 * H, size), :] = value

    lane = lax.broadcasted_iota(jnp.int32, (1, group), 1)
    quads, couls = [], []
    for g in range(width // group):
        quads.append(jnp.where(lane < reals, quad_ref[base + g], quad_ref[base + g + pair]))
        couls.append(jnp.where(lane < reals, coul_ref[base + g], coul_ref[base + g + pair]))
    quad = jnp.concatenate(quads, axis=1)
    coul = jnp.concatenate(couls, axis=1)

    signal = jnp.dot(fwd_ref[...], held_ref[...], preferred_element_type=F32)
    square = signal * signal + small
    inverse = lax.rsqrt(square)
    root = square * inverse
    high, low = split(signal * (quad * root + coul * inverse))
    force_ref[:NT] = high
    force_ref[NT:2 * NT] = high
    force_ref[2 * NT:] = low
    roots = jnp.sum(root, axis=0, keepdims=True)
    inverses = jnp.sum(inverse, axis=0, keepdims=True)
    cubes = jnp.sum(inverse * inverse * inverse, axis=0, keepdims=True)
    mean = (quad * (2.0 * roots - small * inverses) + coul * (small * cubes)) * (1.0 / NT)

    first = pl.multiple_of((me // 2) * 2 * size, 2 * size)
    back = jnp.dot(inv_ref[pl.ds(first, 2 * size), :], force_ref[...], preferred_element_type=F32) * (2.0 * H / NT)
    lower = core == 0
    mine_ref[:size] = jnp.where(lower, back[:size], back[size:])
    other = jnp.where(lower, back[size:], back[:size])
    slope = jnp.broadcast_to(mean, (8, width))
    mine_ref[size:] = slope
    other_ref[...] = other[:harm]
    other_im_ref[:harm] = other[harm:]
    other_im_ref[harm:] = slope


def prepare_kernel(harm, bodies, reals, imped_ref, mine_ref, other_re_ref, other_im_ref, excite_ref, velocity_ref,
                   rest_ref, p_ref, q_ref, vel_ref, slope_ref):
    everyone = imped_ref.shape[3]
    group = 2 * reals
    half = bodies // 2
    pair = bodies // 4
    core = lax.axis_index("harm") % 2
    mine_re_ref, mine_im_ref = mine_ref.at[:harm], mine_ref.at[harm:]
    for which, re_ref, im_ref in ((core, mine_re_ref, mine_im_ref), (1 - core, other_re_ref, other_im_ref)):
        for j in range(pair):
            cols = slice(j * group, (j + 1) * group)
            re = re_ref[:, cols]
            im = im_ref[:harm, cols]
            slope = im_ref[harm:harm + 1, cols]
            one = which * half + j
            two = one + pair
            rest_ref[pl.ds(one, harm, stride=bodies), :] = jnp.concatenate([re[:, :reals], im[:, :reals]], axis=1)
            rest_ref[pl.ds(two, harm, stride=bodies), :] = jnp.concatenate([re[:, reals:], im[:, reals:]], axis=1)
            slope_ref[pl.ds(one, 1), :] = jnp.concatenate([slope[:, :reals], slope[:, :reals]], axis=1)
            slope_ref[pl.ds(two, 1), :] = jnp.concatenate([slope[:, reals:], slope[:, reals:]], axis=1)

    first = lax.axis_index("body") * bodies
    row = lax.broadcasted_iota(jnp.int32, (bodies, everyone), 0)
    col = lax.broadcasted_iota(jnp.int32, (bodies, everyone), 1)
    mine = col == row + first
    ones = jnp.ones((everyone, group), BF16)
    sign = jnp.where(lax.broadcasted_iota(jnp.int32, (bodies, group), 1) < reals, 1.0, -1.0)
    slope = slope_ref[...]
    for h in range(harm):
        rows = pl.ds(h * bodies, bodies)
        rows_im = pl.ds((harm + h) * bodies, bodies)
        real = jnp.where(mine, imped_ref[0, h], jnp.zeros((), BF16))
        imag = jnp.where(mine, imped_ref[1, h], jnp.zeros((), BF16))
        den = jnp.dot(jnp.concatenate([real, imag], axis=0), ones, preferred_element_type=F32)
        den_re = den[:bodies] + slope
        den_im = den[bodies:]
        inverse = 1.0 / (den_re * den_re + den_im * den_im)
        p_ref[rows, :] = den_re * inverse
        q_ref[rows, :] = den_im * inverse * sign
        vel = jnp.concatenate([velocity_ref[rows, :], velocity_ref[rows_im, :]], axis=1)
        vel_ref[rows, :] = vel
        excite = jnp.concatenate([excite_ref[rows, :], excite_ref[rows_im, :]], axis=1)
        rest_ref[rows, :] = rest_ref[rows, :] - excite + slope * (vel - vel.astype(BF16).astype(F32))


def coupling(imped, vels, bodies, reals):
    sign = jnp.where(lax.broadcasted_iota(jnp.int32, (bodies, 2 * reals), 1) < reals, -1.0, 1.0)
    out = jnp.dot(imped.reshape(2 * bodies, imped.shape[2]), vels, preferred_element_type=F32)
    return out[:bodies] + sign * pltpu.roll(out[bodies:], reals, 1)


def at_ends(me):
    return jnp.logical_or(me == 0, me == 3)


def partial_kernel(harm, bodies, reals, imped_ref, own_ref, near_ref, cross_ref, across_ref, rest_ref, out_ref, held_ref):
    me = lax.axis_index("body")
    ends = at_ends(me)
    held_ref[...] = jnp.zeros_like(held_ref)
    for h in range(harm):
        rows = pl.ds(h * bodies, bodies)
        slot = h % 4
        for flip, value in ((0, own_ref[rows, :]), (1, near_ref[rows, :]),
                            (3, jnp.where(ends, across_ref[rows, :], cross_ref[rows, :]))):
            held_ref[slot, pl.ds(pl.multiple_of((me ^ flip) * bodies, bodies), bodies), :] = value
        out_ref[rows, :] = rest_ref[rows, :] + coupling(imped_ref[:, h], held_ref[slot], bodies, reals)


def couple_kernel(harm, bodies, reals, line, imped_ref, *refs):
    pieces, (rest_ref, res_ref, total_ref) = refs[:-3], refs[-3:]
    total = jnp.zeros((8, 2 * reals), F32)
    if line:
        me = lax.axis_index("body")
        ends = at_ends(me)
        source = me ^ 2
        lower = source % 2 == 0
        none = jnp.zeros((bodies, 2 * reals), BF16)
        cols = pl.ds(pl.multiple_of((source // 2) * 2 * bodies, 2 * bodies), 2 * bodies)
    for h in range(harm):
        rows = pl.ds(h * bodies, bodies)
        if line:
            value = jnp.where(ends, pieces[0][rows, :], pieces[1][rows, :])
            vels = jnp.concatenate([jnp.where(lower, value, none), jnp.where(lower, none, value)], axis=0)
            imped = imped_ref[:, h, :, cols]
        else:
            vels = pieces[0][:, h].reshape(-1, 2 * reals)
            imped = imped_ref[:, h]
        res = coupling(imped, vels, bodies, reals) + rest_ref[rows, :]
        res_ref[rows, :] = res
        total = total + jnp.sum((res * res).reshape(bodies // 8, 8, 2 * reals), axis=0)
    total_ref[...] = jnp.broadcast_to(jnp.sum(total), total_ref.shape)


def finish_kernel(harm, bodies, reals, res_ref, p_ref, q_ref, vel_ref, out_ref):
    rows = out_ref.shape[1]
    at = pl.ds(pl.multiple_of(pl.program_id(0) * rows, rows), rows)
    res = res_ref[at, :]
    new = vel_ref[at, :] - (res * p_ref[at, :] + pltpu.roll(res, reals, 1) * q_ref[at, :])
    out_ref[0] = new[:, :reals]
    out_ref[1] = new[:, reals:]


def rms_kernel(scale, *refs):
    *parts, out_ref = refs
    mean = sum(part[...] for part in parts) * scale
    out_ref[0] = jnp.sqrt(mean)[0, 0]


def gather_line(x, axis):
    near = lax.ppermute(x, axis, [(0, 1), (1, 0), (2, 3), (3, 2)])
    cross = lax.ppermute(x, axis, [(1, 2), (2, 1)])
    across = lax.ppermute(x, axis, [(0, 3), (3, 0)])
    outer = lax.ppermute(cross, axis, [(1, 0), (2, 3)])
    inner = lax.ppermute(near, axis, [(1, 2), (2, 1)])
    return x, near, cross, across, outer, inner


def params(mib=24):
    return pltpu.CompilerParams(vmem_limit_bytes=mib << 20)


def cost(flops, moved):
    return pl.CostEstimate(flops=flops, bytes_accessed=moved, transcendentals=0)


def make_local(mesh):
    body_count = mesh.shape["body"]

    def local(vel, imped, excite, quad_coef, coul_coef):
        _, harm, bodies, reals = vel.shape
        everyone = imped.shape[3]
        group = 2 * reals
        total_rows = harm * bodies
        forward, inverse = wave_constants(H // harm)
        flat = vel.reshape(2 * total_rows, reals)
        flat_excite = excite.reshape(2 * total_rows, reals)
        dense = jax.ShapeDtypeStruct((total_rows, group), F32)

        def flipped(x, flip):
            return lax.ppermute(x, "harm", [(i, i ^ flip) for i in range(4)])

        low = pl.pallas_call(
            functools.partial(pack_couple, harm, bodies, reals),
            out_shape=jax.ShapeDtypeStruct((total_rows, group), BF16),
            compiler_params=params(),
            cost_estimate=cost(0, 1 << 10),
            name="pack_couple",
        )(flat)
        columns = bodies * reals // 2
        own, send = pl.pallas_call(
            functools.partial(pack_time, harm, bodies, reals),
            in_specs=[VMEM],
            out_shape=(
                *[jax.ShapeDtypeStruct((2 * harm, columns), BF16)] * 2,
            ),
            compiler_params=params(),
            cost_estimate=cost(0, 1 << 10),
            name="pack_time",
        )(flat)
        if body_count == 4:
            pieces = gather_line(low, "body")
        else:
            pieces = (lax.all_gather(low, "body").reshape(body_count, harm, bodies, group),)

        far = flipped(own, 2)
        far_core = flipped(send, 3)
        core = flipped(send, 1)

        width = 8 * group
        tile = pl.BlockSpec((2 * harm, width), lambda i: (0, i))
        heights = (2 * harm + 8, harm, harm + 8)
        mine, *other = pl.pallas_call(
            functools.partial(time_kernel, harm, bodies, reals),
            grid=(columns // width,),
            in_specs=[SMEM, SMEM, tile, tile, tile, tile, VMEM, VMEM],
            out_specs=[pl.BlockSpec((height, width), lambda i: (0, i)) for height in heights],
            out_shape=tuple(jax.ShapeDtypeStruct((height, columns), F32) for height in heights),
            scratch_shapes=[pltpu.VMEM((4 * H, width), BF16), pltpu.VMEM((3 * NT, width), BF16)],
            compiler_params=params(),
            cost_estimate=cost(0, 1 << 10),
            name="time_kernel",
        )(quad_coef, coul_coef, own, core, far, far_core, jnp.asarray(forward), jnp.asarray(inverse))
        other = [flipped(part, 1) for part in other]

        rest, factor_p, factor_q, vel_dense = pl.pallas_call(
            functools.partial(prepare_kernel, harm, bodies, reals),
            in_specs=[VMEM] * 6,
            out_shape=(dense,) * 4,
            scratch_shapes=[pltpu.VMEM((bodies, group), F32)],
            compiler_params=params(),
            cost_estimate=cost(0, 1 << 10),
            name="prepare",
        )(imped, mine, *other, flat_excite, flat)

        if body_count == 4:
            rest = pl.pallas_call(
                functools.partial(partial_kernel, harm, bodies, reals),
                in_specs=[VMEM] * 6,
                out_shape=dense,
                scratch_shapes=[pltpu.VMEM((4, everyone, group), BF16)],
                compiler_params=params(),
                cost_estimate=cost(0, 1 << 10),
                name="partial",
            )(imped, *pieces[:4], rest)
            pieces = pieces[4:]
        res, total = pl.pallas_call(
            functools.partial(couple_kernel, harm, bodies, reals, body_count == 4),
            in_specs=[VMEM] * (2 + len(pieces)),
            out_shape=(dense, jax.ShapeDtypeStruct((8, 128), F32)),
            compiler_params=params(),
            cost_estimate=cost(0, 1 << 10),
            name="couple",
        )(imped, *pieces, rest)

        steps = 2
        rows = total_rows // steps
        new = pl.pallas_call(
            functools.partial(finish_kernel, harm, bodies, reals),
            grid=(steps,),
            in_specs=[VMEM] * 4,
            out_specs=pl.BlockSpec((2, rows, reals), lambda i: (0, i, 0)),
            out_shape=jax.ShapeDtypeStruct((2, total_rows, reals), F32),
            compiler_params=params(),
            cost_estimate=cost(0, 1 << 10),
            name="finish",
        )(res, factor_p, factor_q, vel_dense)

        total = total + sum(flipped(total, flip) for flip in (3, 2, 1))

        def crossed(flip):
            pairs = [(4 * i + j, 4 * (i ^ flip) + (j ^ 1)) for i in range(body_count) for j in range(4)]
            return lax.ppermute(total, ("body", "harm"), pairs)

        for bit in range(2, body_count.bit_length() - 1):
            total = total + crossed(1 << bit)
        got = [crossed(flip) for flip in (3, 2, 1)]
        rms = pl.pallas_call(
            functools.partial(rms_kernel, 1.0 / (2.0 * H * everyone * reals)),
            in_specs=[VMEM] * (1 + len(got)),
            out_specs=SMEM,
            out_shape=jax.ShapeDtypeStruct((1,), F32),
            compiler_params=params(),
            name="rms",
        )(total, *got)
        return new.reshape(vel.shape), rms

    return local


def solution(mesh):
    in_specs = (
        P(None, "harm", "body", "sea"),
        P(None, "harm", "body", None),
        P(None, "harm", "body", "sea"),
        P("body"),
        P("body"),
    )
    out_specs = (P(None, "harm", "body", "sea"), P("sea"))
    return jax.shard_map(make_local(mesh), mesh=mesh, in_specs=in_specs, out_specs=out_specs, check_vma=False)
```

```python
import functools
import math

import ml_dtypes
import numpy as np
import jax
import jax.numpy as jnp
from jax import lax
from jax.experimental import pallas as pl
from jax.experimental.pallas import tpu as pltpu
from jax.sharding import PartitionSpec as P

H = 128
NT = 512
DELTA = 0.1
F32 = jnp.float32
BF16 = jnp.bfloat16
VMEM = pl.BlockSpec(memory_space=pltpu.VMEM)
SMEM = pl.BlockSpec(memory_space=pltpu.SMEM)


def split(x):
    high = x.astype(BF16)
    return high, (x - high.astype(F32)).astype(BF16)


def wave_constants(groups):
    k = np.arange(1, H + 1)
    phase = np.arange(NT)[None, :] * k[:, None] % NT
    angle = phase * (2.0 * math.pi / NT)
    waves = np.stack([np.cos(angle), -np.sin(angle)]).reshape(2, groups, H // groups, NT)
    table = (np.swapaxes(waves, 0, 1).reshape(2 * H, NT) / math.sqrt(H)).astype(np.float32)
    high = table.astype(ml_dtypes.bfloat16)
    low = (table - high.astype(np.float32)).astype(ml_dtypes.bfloat16)
    return np.concatenate([high.T, low.T], axis=1), np.concatenate([high, low, high], axis=1)


def pack_couple(harm, bodies, reals, vel_ref, out_ref):
    for h in range(harm):
        rows = pl.ds(h * bodies, bodies)
        re = vel_ref[rows, :]
        im = vel_ref[pl.ds((harm + h) * bodies, bodies), :]
        out_ref[rows, :] = jnp.concatenate([re, im], axis=1).astype(BF16)


def pack_time(harm, bodies, reals, vel_ref, own_ref, send_ref, again_ref):
    core = lax.axis_index("harm") % 2
    half = bodies // 2
    pair = bodies // 4
    for which, out_ref in ((core, own_ref), (1 - core, send_ref)):
        for j in range(pair):
            one = vel_ref[pl.ds(which * half + j, 2 * harm, stride=bodies), :]
            two = vel_ref[pl.ds(which * half + pair + j, 2 * harm, stride=bodies), :]
            out_ref[:, pl.ds(j * 2 * reals, 2 * reals)] = jnp.concatenate([one, two], axis=1).astype(BF16)
    pack_couple(harm, bodies, reals, vel_ref, again_ref)


def time_kernel(harm, bodies, reals, quad_ref, coul_ref, own_ref, core_ref, far_ref, far_core_ref, fwd_ref, inv_ref,
                mine_ref, other_ref, other_im_ref, held_ref, force_ref):
    step = pl.program_id(0)
    me = lax.axis_index("harm")
    core = me % 2
    size = 2 * harm
    width = own_ref.shape[1]
    group = 2 * reals
    pair = bodies // 4
    base = core * (bodies // 2) + step * (width // group)
    small = DELTA * DELTA

    for flip, ref in enumerate((own_ref, core_ref, far_ref, far_core_ref)):
        value = ref[...]
        first = pl.multiple_of((me ^ flip) * size, size)
        held_ref[pl.ds(first, size), :] = value
        held_ref[pl.ds(first + 2 * H, size), :] = value

    lane = lax.broadcasted_iota(jnp.int32, (1, group), 1)
    quads, couls = [], []
    for g in range(width // group):
        quads.append(jnp.where(lane < reals, quad_ref[base + g], quad_ref[base + g + pair]))
        couls.append(jnp.where(lane < reals, coul_ref[base + g], coul_ref[base + g + pair]))
    quad = jnp.concatenate(quads, axis=1)
    coul = jnp.concatenate(couls, axis=1)

    signal = jnp.dot(fwd_ref[...], held_ref[...], preferred_element_type=F32)
    square = signal * signal + small
    inverse = lax.rsqrt(square)
    root = square * inverse
    high, low = split(signal * (quad * root + coul * inverse))
    force_ref[:NT] = high
    force_ref[NT:2 * NT] = high
    force_ref[2 * NT:] = low
    roots = jnp.sum(root, axis=0, keepdims=True)
    inverses = jnp.sum(inverse, axis=0, keepdims=True)
    cubes = jnp.sum(inverse * inverse * inverse, axis=0, keepdims=True)
    mean = (quad * (2.0 * roots - small * inverses) + coul * (small * cubes)) * (1.0 / NT)

    first = pl.multiple_of((me // 2) * 2 * size, 2 * size)
    back = jnp.dot(inv_ref[pl.ds(first, 2 * size), :], force_ref[...], preferred_element_type=F32) * (2.0 * H / NT)
    lower = core == 0
    mine_ref[:size] = jnp.where(lower, back[:size], back[size:])
    other = jnp.where(lower, back[size:], back[:size])
    slope = jnp.broadcast_to(mean, (8, width))
    mine_ref[size:] = slope
    other_ref[...] = other[:harm]
    other_im_ref[:harm] = other[harm:]
    other_im_ref[harm:] = slope


def prepare_kernel(harm, bodies, reals, imped_ref, mine_ref, other_re_ref, other_im_ref, excite_ref, velocity_ref,
                   rest_ref, p_ref, q_ref, vel_ref, slope_ref):
    everyone = imped_ref.shape[3]
    group = 2 * reals
    half = bodies // 2
    pair = bodies // 4
    core = lax.axis_index("harm") % 2
    mine_re_ref, mine_im_ref = mine_ref.at[:harm], mine_ref.at[harm:]
    for which, re_ref, im_ref in ((core, mine_re_ref, mine_im_ref), (1 - core, other_re_ref, other_im_ref)):
        for j in range(pair):
            cols = slice(j * group, (j + 1) * group)
            re = re_ref[:, cols]
            im = im_ref[:harm, cols]
            slope = im_ref[harm:harm + 1, cols]
            one = which * half + j
            two = one + pair
            rest_ref[pl.ds(one, harm, stride=bodies), :] = jnp.concatenate([re[:, :reals], im[:, :reals]], axis=1)
            rest_ref[pl.ds(two, harm, stride=bodies), :] = jnp.concatenate([re[:, reals:], im[:, reals:]], axis=1)
            slope_ref[pl.ds(one, 1), :] = jnp.concatenate([slope[:, :reals], slope[:, :reals]], axis=1)
            slope_ref[pl.ds(two, 1), :] = jnp.concatenate([slope[:, reals:], slope[:, reals:]], axis=1)

    first = lax.axis_index("body") * bodies
    row = lax.broadcasted_iota(jnp.int32, (bodies, everyone), 0)
    col = lax.broadcasted_iota(jnp.int32, (bodies, everyone), 1)
    mine = col == row + first
    ones = jnp.ones((everyone, group), BF16)
    sign = jnp.where(lax.broadcasted_iota(jnp.int32, (bodies, group), 1) < reals, 1.0, -1.0)
    slope = slope_ref[...]
    for h in range(harm):
        rows = pl.ds(h * bodies, bodies)
        rows_im = pl.ds((harm + h) * bodies, bodies)
        real = jnp.where(mine, imped_ref[0, h], jnp.zeros((), BF16))
        imag = jnp.where(mine, imped_ref[1, h], jnp.zeros((), BF16))
        den = jnp.dot(jnp.concatenate([real, imag], axis=0), ones, preferred_element_type=F32)
        den_re = den[:bodies] + slope
        den_im = den[bodies:]
        inverse = 1.0 / (den_re * den_re + den_im * den_im)
        p_ref[rows, :] = den_re * inverse
        q_ref[rows, :] = den_im * inverse * sign
        vel = jnp.concatenate([velocity_ref[rows, :], velocity_ref[rows_im, :]], axis=1)
        vel_ref[rows, :] = vel
        excite = jnp.concatenate([excite_ref[rows, :], excite_ref[rows_im, :]], axis=1)
        rest_ref[rows, :] = rest_ref[rows, :] - excite + slope * (vel - vel.astype(BF16).astype(F32))


def coupling(imped, vels, bodies, reals):
    sign = jnp.where(lax.broadcasted_iota(jnp.int32, (bodies, 2 * reals), 1) < reals, -1.0, 1.0)
    out = jnp.dot(imped.reshape(2 * bodies, imped.shape[2]), vels, preferred_element_type=F32)
    return out[:bodies] + sign * pltpu.roll(out[bodies:], reals, 1)


def at_ends(me):
    return jnp.logical_or(me == 0, me == 3)


def partial_kernel(harm, bodies, reals, imped_ref, own_ref, near_ref, cross_ref, across_ref, rest_ref, out_ref, held_ref):
    me = lax.axis_index("body")
    ends = at_ends(me)
    held_ref[...] = jnp.zeros_like(held_ref)
    for h in range(harm):
        rows = pl.ds(h * bodies, bodies)
        slot = h % 4
        for flip, value in ((0, own_ref[rows, :]), (1, near_ref[rows, :]),
                            (3, jnp.where(ends, across_ref[rows, :], cross_ref[rows, :]))):
            held_ref[slot, pl.ds(pl.multiple_of((me ^ flip) * bodies, bodies), bodies), :] = value
        out_ref[rows, :] = rest_ref[rows, :] + coupling(imped_ref[:, h], held_ref[slot], bodies, reals)


def couple_kernel(harm, bodies, reals, line, imped_ref, *refs):
    pieces, (rest_ref, res_ref, total_ref) = refs[:-3], refs[-3:]
    total = jnp.zeros((8, 2 * reals), F32)
    if line:
        me = lax.axis_index("body")
        ends = at_ends(me)
        source = me ^ 2
        lower = source % 2 == 0
        none = jnp.zeros((bodies, 2 * reals), BF16)
        cols = pl.ds(pl.multiple_of((source // 2) * 2 * bodies, 2 * bodies), 2 * bodies)
    for h in range(harm):
        rows = pl.ds(h * bodies, bodies)
        if line:
            value = jnp.where(ends, pieces[0][rows, :], pieces[1][rows, :])
            vels = jnp.concatenate([jnp.where(lower, value, none), jnp.where(lower, none, value)], axis=0)
            imped = imped_ref[:, h, :, cols]
        else:
            vels = pieces[0][:, h].reshape(-1, 2 * reals)
            imped = imped_ref[:, h]
        res = coupling(imped, vels, bodies, reals) + rest_ref[rows, :]
        res_ref[rows, :] = res
        total = total + jnp.sum((res * res).reshape(bodies // 8, 8, 2 * reals), axis=0)
    total_ref[...] = jnp.broadcast_to(jnp.sum(total), total_ref.shape)


def finish_kernel(harm, bodies, reals, res_ref, p_ref, q_ref, vel_ref, out_ref):
    rows = out_ref.shape[1]
    at = pl.ds(pl.multiple_of(pl.program_id(0) * rows, rows), rows)
    res = res_ref[at, :]
    new = vel_ref[at, :] - (res * p_ref[at, :] + pltpu.roll(res, reals, 1) * q_ref[at, :])
    out_ref[0] = new[:, :reals]
    out_ref[1] = new[:, reals:]


def rms_kernel(scale, *refs):
    *parts, out_ref = refs
    mean = sum(part[...] for part in parts) * scale
    out_ref[...] = jnp.sqrt(mean)[:1, :1]


def gather_line(x, again, axis):
    near = lax.ppermute(x, axis, [(0, 1), (1, 0), (2, 3), (3, 2)])
    cross = lax.ppermute(x, axis, [(1, 2), (2, 1)])
    across = lax.ppermute(again, axis, [(0, 3), (3, 0)])
    outer = lax.ppermute(cross, axis, [(1, 0), (2, 3)])
    inner = lax.ppermute(near, axis, [(1, 2), (2, 1)])
    return x, near, cross, across, outer, inner


def params(mib=24):
    return pltpu.CompilerParams(vmem_limit_bytes=mib << 20)


def cost(flops, moved):
    return pl.CostEstimate(flops=flops, bytes_accessed=moved, transcendentals=0)


def make_local(mesh):
    body_count = mesh.shape["body"]

    def local(vel, imped, excite, quad_coef, coul_coef):
        _, harm, bodies, reals = vel.shape
        everyone = imped.shape[3]
        group = 2 * reals
        total_rows = harm * bodies
        forward, inverse = wave_constants(H // harm)
        flat = vel.reshape(2 * total_rows, reals)
        flat_excite = excite.reshape(2 * total_rows, reals)
        dense = jax.ShapeDtypeStruct((total_rows, group), F32)

        def flipped(x, flip):
            return lax.ppermute(x, "harm", [(i, i ^ flip) for i in range(4)])

        low = pl.pallas_call(
            functools.partial(pack_couple, harm, bodies, reals),
            out_shape=jax.ShapeDtypeStruct((total_rows, group), BF16),
            compiler_params=params(),
            cost_estimate=cost(0, 1 << 10),
            name="pack_couple",
        )(flat)
        columns = bodies * reals // 2
        own, send, again = pl.pallas_call(
            functools.partial(pack_time, harm, bodies, reals),
            in_specs=[VMEM],
            out_shape=(
                *[jax.ShapeDtypeStruct((2 * harm, columns), BF16)] * 2,
                jax.ShapeDtypeStruct((total_rows, group), BF16),
            ),
            compiler_params=params(),
            cost_estimate=cost(0, 1 << 10),
            name="pack_time",
        )(flat)
        if body_count == 4:
            pieces = gather_line(low, again, "body")
        else:
            pieces = (lax.all_gather(low, "body").reshape(body_count, harm, bodies, group),)

        far = flipped(own, 2)
        far_core = flipped(send, 3)
        core = flipped(send, 1)

        width = 8 * group
        tile = pl.BlockSpec((2 * harm, width), lambda i: (0, i))
        heights = (2 * harm + 8, harm, harm + 8)
        mine, *other = pl.pallas_call(
            functools.partial(time_kernel, harm, bodies, reals),
            grid=(columns // width,),
            in_specs=[SMEM, SMEM, tile, tile, tile, tile, VMEM, VMEM],
            out_specs=[pl.BlockSpec((height, width), lambda i: (0, i)) for height in heights],
            out_shape=tuple(jax.ShapeDtypeStruct((height, columns), F32) for height in heights),
            scratch_shapes=[pltpu.VMEM((4 * H, width), BF16), pltpu.VMEM((3 * NT, width), BF16)],
            compiler_params=params(),
            cost_estimate=cost(0, 1 << 10),
            name="time_kernel",
        )(quad_coef, coul_coef, own, core, far, far_core, jnp.asarray(forward), jnp.asarray(inverse))
        other = [flipped(part, 1) for part in other]

        rest, factor_p, factor_q, vel_dense = pl.pallas_call(
            functools.partial(prepare_kernel, harm, bodies, reals),
            in_specs=[VMEM] * 6,
            out_shape=(dense,) * 4,
            scratch_shapes=[pltpu.VMEM((bodies, group), F32)],
            compiler_params=params(),
            cost_estimate=cost(0, 1 << 10),
            name="prepare",
        )(imped, mine, *other, flat_excite, flat)

        if body_count == 4:
            rest = pl.pallas_call(
                functools.partial(partial_kernel, harm, bodies, reals),
                in_specs=[VMEM] * 6,
                out_shape=dense,
                scratch_shapes=[pltpu.VMEM((4, everyone, group), BF16)],
                compiler_params=params(),
                cost_estimate=cost(0, 1 << 10),
                name="partial",
            )(imped, *pieces[:4], rest)
            pieces = pieces[4:]
        res, total = pl.pallas_call(
            functools.partial(couple_kernel, harm, bodies, reals, body_count == 4),
            in_specs=[VMEM] * (2 + len(pieces)),
            out_shape=(dense, jax.ShapeDtypeStruct((8, 128), F32)),
            compiler_params=params(),
            cost_estimate=cost(0, 1 << 10),
            name="couple",
        )(imped, *pieces, rest)

        steps = 2
        rows = total_rows // steps
        new = pl.pallas_call(
            functools.partial(finish_kernel, harm, bodies, reals),
            grid=(steps,),
            in_specs=[VMEM] * 4,
            out_specs=pl.BlockSpec((2, rows, reals), lambda i: (0, i, 0)),
            out_shape=jax.ShapeDtypeStruct((2, total_rows, reals), F32),
            compiler_params=params(),
            cost_estimate=cost(0, 1 << 10),
            name="finish",
        )(res, factor_p, factor_q, vel_dense)

        total = total + flipped(total, 1)
        total = total + flipped(total, 3)

        def crossed(flip):
            pairs = [(4 * i + j, 4 * (i ^ flip) + (j ^ 1)) for i in range(body_count) for j in range(4)]
            return lax.ppermute(total, ("body", "harm"), pairs)

        for bit in range(2, body_count.bit_length() - 1):
            total = total + crossed(1 << bit)
        got = [crossed(flip) for flip in (3, 2, 1)]
        rms = pl.pallas_call(
            functools.partial(rms_kernel, 1.0 / (2.0 * H * everyone * reals)),
            in_specs=[VMEM] * (1 + len(got)),
            out_specs=VMEM,
            out_shape=jax.ShapeDtypeStruct((1, 1), F32),
            compiler_params=params(),
            name="rms",
        )(total, *got)
        return new.reshape(vel.shape), rms.reshape(1)

    return local


def solution(mesh):
    in_specs = (
        P(None, "harm", "body", "sea"),
        P(None, "harm", "body", None),
        P(None, "harm", "body", "sea"),
        P("body"),
        P("body"),
    )
    out_specs = (P(None, "harm", "body", "sea"), P("sea"))
    return jax.shard_map(make_local(mesh), mesh=mesh, in_specs=in_specs, out_specs=out_specs, check_vma=False)
```
